512 devices in a mesh: mem: 8 (over z_lo), space: 64 (over z_hi, x, y, core).
Axes of the slice: x: 4, y: 4, z: 16 (z_hi: 2, z_lo: 8; z = z_hi * 8 + z_lo), core: 2. Of those that a mesh axis runs over, the one named last changes fastest.
Arguments:
- gradient: bfloat16 [6, 2, 768, 1536], P(None, None, 'space', 'mem'), may hold values from -6 to 6
- perturbations: bfloat16 [16, 6, 2, 768, 1536], P('mem', None, None, 'space'), may hold values from -6 to 6
- band_index: int32 [768, 1536], P('space'), may hold values from 0 to 15
- band_weight: float32 [16], replicated, may hold values from 0.3 to 3
- wave_index: int32 [768, 768], P('space'), may hold values from 0 to 767
- spectrum: float32 [2, 768], replicated, may hold values from 0.3 to 3
Outputs:
- control_grad: float32 [16, 2, 1536, 768], P('mem', None, 'space')
The draws below stay inside these ranges and needn't reach their ends.
All inputs are finite; a program needn't handle non-finite values.
Results may differ from the reference program's by a relative error of at most 0.0058.
Values may be sent and summed in bfloat16 or wider, within the bound.
A program may use at most 64 MiB of HBM per device.

```python
import math
import jax
import jax.numpy as jnp
from jax import lax

F = 6
LEV = 2
NLAT = 768
NLON = 1536
MT = 768
NDEG = 768
NBAND = 16
MEM = 16


def with_ends(result, rng, smallest, high):
    spot = [jax.random.randint(jax.random.fold_in(rng, axis), (), 0, length) for axis, length in enumerate(result.shape)]
    widest = result.shape.index(max(result.shape))
    neighbour = spot[:widest] + [(spot[widest] + 1) % result.shape[widest]] + spot[widest + 1:]
    return result.at[tuple(spot)].set(smallest).at[tuple(neighbour)].set(high)


def levels(stream_key, shape, shards, smallest, largest):
    def one(axis_at, shards_of):
        draws = jax.random.uniform(jax.random.fold_in(jax.random.fold_in(stream_key, 6), axis_at), (shards_of,), jnp.float32, smallest / len(shards), largest / len(shards))
        return jnp.repeat(jnp.exp(draws), shape[axis_at] // shards_of).reshape((-1,) + (1,) * (len(shape) - axis_at - 1))

    level = one(*shards[0])
    for cut in shards[1:]:
        level = level * one(*cut)
    return level


def gaussian(own_key, shape, spread, most, cuts=(), held_as=jnp.bfloat16):
    array = spread * jax.random.normal(own_key, shape, jnp.float32)
    if cuts:
        array = array * levels(own_key, shape, cuts, -0.22, 0.18)
    return jnp.clip(array, -most, most).astype(held_as)


def setup_inputs(seed: int = 0) -> dict:
    keys = jax.random.split(jax.random.key(seed), 7)
    gradient = gaussian(keys[0], (F, LEV, NLAT, NLON), 1.0, 6.0, ((2, 64), (3, 8)))
    perturbations = gaussian(keys[1], (MEM, F, LEV, NLAT, NLON), 1.0, 6.0, ((0, 8), (3, 64)))
    band_index = with_ends(jax.random.randint(keys[2], (NLAT, NLON), 0, NBAND), jax.random.fold_in(keys[2], 1), 0, NBAND - 1).astype(jnp.int32)
    band_weight = jnp.clip(jnp.exp(jax.random.uniform(keys[3], (NBAND,), jnp.float32, math.log(0.3), math.log(3.0))), 0.3, 3.0)
    wave_index = with_ends(jax.random.randint(keys[4], (MT, NDEG), 0, NDEG), jax.random.fold_in(keys[4], 1), 0, NDEG - 1).astype(jnp.int32)
    spectrum = jnp.clip(jnp.exp(jax.random.uniform(keys[5], (LEV, NDEG), jnp.float32, math.log(0.3), math.log(3.0))), 0.3, 3.0)
    return {"gradient": gradient, "perturbations": perturbations, "band_index": band_index, "band_weight": band_weight, "wave_index": wave_index, "spectrum": spectrum}


def zonal_table(nlon, waves):
    lon_index = jnp.arange(nlon, dtype=jnp.int32)[:, None]
    column = jnp.arange(2 * waves, dtype=jnp.int32)[None, :]
    wavenumber = column // 2
    phase = lon_index * wavenumber % nlon
    angle = phase.astype(jnp.float32) * jnp.float32(2.0 * math.pi / nlon)
    values = jnp.where(column % 2 == 0, jnp.cos(angle), -jnp.sin(angle))
    return (values * jnp.float32(math.sqrt(2.0 / nlon))).astype(jnp.bfloat16)

def latitude_basis(nlat, degrees):
    cycle = jnp.arange(nlat, dtype=jnp.int32)[:, None]
    degree = jnp.arange(degrees, dtype=jnp.int32)[None, :]
    phase = degree * (2 * cycle + 1) % (4 * nlat)
    angle = phase.astype(jnp.float32) * jnp.float32(math.pi / (2 * nlat))
    return (jnp.cos(angle) * jnp.float32(math.sqrt(2.0 / nlat))).astype(jnp.bfloat16)

def reference(gradient, perturbations, band_index, band_weight, wave_index, spectrum):
    area = band_weight[band_index].astype(jnp.float32)
    table = zonal_table(NLON, MT)
    basis = latitude_basis(NLAT, NDEG).astype(jnp.float32)
    factor = jnp.repeat(spectrum[:, wave_index], 2, axis=1).astype(jnp.float32)
    grad_float = gradient.astype(jnp.float32)

    def member_term(member_pert):
        alpha_grad = (area * lax.optimization_barrier(jnp.sum(member_pert.astype(jnp.float32) * grad_float, axis=0))).astype(jnp.bfloat16)
        zonal_terms = jnp.dot(alpha_grad.reshape(LEV * NLAT, NLON), table, preferred_element_type=jnp.float32)
        zonal_terms = zonal_terms.astype(jnp.bfloat16).reshape(LEV, NLAT, 2 * MT).astype(jnp.float32)
        summed = jnp.einsum('ljq,jk->lqk', zonal_terms, basis)
        return summed * factor
    return lax.map(member_term, perturbations)
```

```python
import functools
import math

import jax
import jax.numpy as jnp
import ml_dtypes
import numpy as np
from jax import lax
from jax.experimental import pallas as pl
from jax.experimental.pallas import tpu as pltpu
from jax.sharding import PartitionSpec as P

MESH = pl.DeviceIdType.MESH
BF16 = jnp.bfloat16
F32 = jnp.float32

MEMS = 8
HALF = 32
NLAT = 768
NLON = 1536
MT = 768
NDEG = 768
CYC = 12
FIELDS = 6
ROWS = 144
GROWS = 224

def gather_trees():
    trees = []
    for s in range(MEMS):
        tree = {n: [] for n in range(MEMS)}
        near = range(0, 4) if s < 4 else range(4, 8)
        relay = s + 4 if s < 4 else s - 4
        far = range(4, 8) if s < 4 else range(0, 4)
        tree[s] = [relay] + sorted((n for n in near if n != s), key=lambda n: -abs(n - s))
        tree[relay] = sorted((n for n in far if n != relay), key=lambda n: -abs(n - relay))
        trees.append(tree)
    return trees


def zonal_constant():
    phase = (np.arange(NLON)[:, None] * np.arange(MT)[None, :]) % NLON
    angle = phase * (2.0 * math.pi / NLON)
    pair = np.stack([np.cos(angle), -np.sin(angle)], axis=-1).reshape(NLON, 2 * MT)
    pair = (pair * math.sqrt(2.0 / NLON)).astype(np.float32).astype(ml_dtypes.bfloat16)
    return np.ascontiguousarray(pair.reshape(NLON, 2, MT).transpose(1, 0, 2))


def latitude_constant():
    phase = (np.arange(NDEG)[None, :] * (2 * np.arange(NLAT)[:, None] + 1)) % (4 * NLAT)
    basis = np.cos(phase * (math.pi / (2 * NLAT))) * math.sqrt(2.0 / NLAT)
    padded = np.zeros((2, HALF, 16, NDEG), np.float32)
    padded[:, :, :CYC] = basis.reshape(2, HALF, CYC, NDEG)
    return padded.reshape(2, HALF * 16, NDEG).astype(ml_dtypes.bfloat16)


def spread_constant():
    place = np.zeros((HALF * 24, HALF * 32), np.float32)
    for d in range(HALF):
        place[d * 24 + np.arange(24), d * 32 + np.arange(24)] = 1.0
    return place.astype(ml_dtypes.bfloat16)


def kernel(
    trees,
    weight_s, grad_h, pert_h, band_h, wave_h, spec_h, table_h, basis_h, place_h,
    out_ref,
    grad_v, pert_v, band_v, wave_v, spec_v, table_v, basis_v, place_v,
    gpack, ppack, area, factor, gbuf, alpha, zsend, zrecv, send, recv,
    load_sem, gs_sem, gr_sem, as_sem, ar_sem, bs_sem, br_sem,
):
    m = lax.axis_index("mem")
    space = lax.axis_index("space")
    zh = space // HALF
    s32 = space % HALF
    partner = (1 - zh) * HALF + s32

    loads = [
        (grad_h, grad_v), (pert_h, pert_v), (band_h, band_v), (wave_h, wave_v), (spec_h, spec_v),
        (table_h.at[1 - zh], table_v.at[0]), (table_h.at[zh], table_v.at[1]), (place_h, place_v),
        (basis_h, basis_v),
    ]
    loads = [pltpu.make_async_copy(a, b, load_sem.at[i]) for i, (a, b) in enumerate(loads)]
    for c in loads:
        c.start()

    barrier = pltpu.get_barrier_semaphore()

    def greet(d, _):
        pl.semaphore_signal(barrier, inc=1, device_id=((m + d) % MEMS, space), device_id_type=MESH)
        return 0

    lax.fori_loop(1, MEMS, greet, 0)
    pl.semaphore_signal(barrier, inc=1, device_id=(m, partner), device_id_type=MESH)

    def greet_half(d, _):
        pl.semaphore_signal(
            barrier, inc=1, device_id=(m, zh * HALF + (s32 + d) % HALF), device_id_type=MESH
        )
        return 0

    lax.fori_loop(1, HALF, greet_half, 0)

    loads[0].wait()
    for f in range(FIELDS):
        for l in range(2):
            v = grad_v[f, l].astype(F32)
            gpack[f * 24 + 8 * l : f * 24 + 8 * l + 8, 0:192] = v[0:8]
            gpack[f * 24 + 16 + 4 * l : f * 24 + 20 + 4 * l, 0:192] = v[8:12]
    lane = lax.broadcasted_iota(jnp.int32, (ROWS, 128), 1)
    low = lane < 64
    t0 = gpack[:, 0:128]
    t1 = gpack[:, 128:256]
    odd = m % 2
    full = jnp.where(odd == 1, jnp.where(low, pltpu.roll(t0, 64, 1), pltpu.roll(t1, 64, 1)), t0)
    part = jnp.where(odd == 1, t0, t1)
    turned = pltpu.roll(part, 64, 1)
    low72 = low[0:72]
    folded = jnp.where(
        odd == 1,
        jnp.where(low72, part[72:144], turned[0:72]),
        jnp.where(low72, part[0:72], turned[72:144]),
    )
    gbuf[m, 0:144] = full.astype(BF16)
    gbuf[m, 144:224] = jnp.concatenate([folded, jnp.zeros((8, 128), F32)], axis=0).astype(BF16)

    pl.semaphore_wait(barrier, MEMS - 1 + 1 + HALF - 1)

    def gather_copy(s, child, index):
        return pltpu.make_async_remote_copy(
            gbuf.at[s], gbuf.at[s], gs_sem.at[index], gr_sem.at[s],
            device_id=(child, space), device_id_type=MESH,
        )

    first = [[(k, c) for c in trees[k][k]] for k in range(MEMS)]
    later = []
    for k in range(MEMS):
        order = sorted((s for s in range(MEMS) if s != k), key=lambda s: (s not in near_of(trees, k), abs(s - k)))
        later.append(order)

    for k in range(MEMS):
        @pl.when(m == k)
        def _(k=k):
            for i, (s, c) in enumerate(first[k]):
                gather_copy(s, c, i).start()

    loads[2].wait()
    band = band_v[...]
    a = jnp.zeros((CYC, NLON), F32)
    for b in range(16):
        a = jnp.where(band == b, weight_s[b], a)
    area[0:8] = a[0:8]
    area[8:16] = a[0:8]
    area[16:20] = a[8:12]
    area[20:24] = a[8:12]

    loads[1].wait()
    for e in range(2):
        for f in range(FIELDS):
            for l in range(2):
                v = pert_v[e, f, l].astype(F32)
                ppack[e, f * 24 + 8 * l : f * 24 + 8 * l + 8] = v[0:8]
                ppack[e, f * 24 + 16 + 4 * l : f * 24 + 20 + 4 * l] = v[8:12]

    loads[3].wait()
    loads[4].wait()
    for t in range(6):
        idx = wave_v[:, t * 128 : t * 128 + 128]
        block = idx // 128
        place = idx % 128
        for l in range(2):
            got = jnp.zeros((CYC, 128), F32)
            for b in range(6):
                row = jnp.broadcast_to(spec_v[l : l + 1, b * 128 : b * 128 + 128], (CYC, 128))
                got = jnp.where(block == b, jnp.take_along_axis(row, place, axis=1), got)
            for r in range(CYC):
                factor[l, 2 * r : 2 * r + 2, t * 128 : t * 128 + 128] = jnp.broadcast_to(
                    got[r : r + 1], (2, 128)
                )

    for k in range(MEMS):
        @pl.when(m == k)
        def _(k=k):
            sent = list(first[k])
            for s in later[k]:
                gather_copy(s, 0, 0).wait_recv()
                for c in trees[s][k]:
                    gather_copy(s, c, len(sent)).start()
                    sent.append((s, c))
            for i, (s, c) in enumerate(sent):
                gather_copy(s, c, i).wait_send()

    low = low72
    for p in range(4):
        ge = gbuf[2 * p].astype(F32)
        go = gbuf[2 * p + 1].astype(F32)
        fe, fo = ge[144:216], go[144:216]
        mid = jnp.concatenate(
            [jnp.where(low, fe, fo), pltpu.roll(jnp.where(low, fo, fe), 64, 1)], axis=0
        )
        for t, tile in enumerate((ge[0:144], mid, go[0:144])):
            lanes = slice((3 * p + t) * 128, (3 * p + t) * 128 + 128)
            rows = []
            for e in range(2):
                acc = ppack[e, 0:24, lanes] * tile[0:24]
                for f in range(1, FIELDS):
                    acc = acc + ppack[e, f * 24 : f * 24 + 24, lanes] * tile[f * 24 : f * 24 + 24]
                rows.append(area[:, lanes] * acc)
            alpha[:, lanes] = jnp.concatenate(rows, axis=0).astype(BF16)

    loads[5].wait()
    zsend[...] = jnp.dot(alpha[...], table_v[0], preferred_element_type=F32).astype(BF16)
    across = pltpu.make_async_remote_copy(
        zsend, zrecv, as_sem, ar_sem, device_id=(m, partner), device_id_type=MESH
    )
    across.start()
    loads[6].wait()
    mine = jnp.dot(alpha[...], table_v[1], preferred_element_type=F32).astype(BF16)

    lane = lax.broadcasted_iota(jnp.int32, (16, 128), 1)
    sub = lax.broadcasted_iota(jnp.int32, (8, 128), 0)

    def message(zs, peer):
        return pltpu.make_async_remote_copy(
            send.at[zs, peer], recv.at[zs, s32], bs_sem.at[zs], br_sem.at[zs],
            device_id=(m, zh * HALF + peer), device_id_type=MESH,
        )

    def spread(z, zs):
        y = jnp.dot(z, place_v[...], preferred_element_type=F32)
        for t in range(8):
            yt = y[:, t * 128 : t * 128 + 128]
            blocks = []
            for e in range(2):
                for l in range(2):
                    top = yt[(3 * e + l) * 8 : (3 * e + l) * 8 + 8]
                    rest = yt[(3 * e + 2) * 8 : (3 * e + 2) * 8 + 8]
                    if l == 1:
                        rest = pltpu.roll(rest, 4, 0)
                    rest = jnp.where(sub < 4, rest, 0.0)
                    blocks.append(jnp.concatenate([top, rest], axis=0))
            for d in range(4):
                whole = None
                for el in range(4):
                    shift = (32 * (el - d)) % 128
                    moved = pltpu.roll(blocks[el], shift, 1) if shift else blocks[el]
                    whole = moved if whole is None else jnp.where(lane >= 32 * el, moved, whole)
                send[zs, 4 * t + d] = whole.astype(BF16)
        recv[zs, s32] = send[zs, s32]

        def go(d, _):
            message(zs, (s32 + d) % HALF).start()
            return 0

        lax.fori_loop(1, HALF, go, 0)

    def arrived(zs):
        pltpu.make_async_copy(send.at[zs, 0:31], recv.at[zs, 0:31], br_sem.at[zs]).wait()

    def left(zs):
        pltpu.make_async_copy(send.at[zs, 0:31], recv.at[zs, 0:31], bs_sem.at[zs]).wait()

    loads[7].wait()
    spread(mine, zh)
    across.wait_recv()
    spread(zrecv[...], 1 - zh)

    loads[8].wait()
    arrived(zh)
    dims = (((0,), (0,)), ((), ()))
    total = lax.dot_general(
        recv[zh].reshape(HALF * 16, 128), basis_v[zh], dims, preferred_element_type=F32
    )
    arrived(1 - zh)
    total = total + lax.dot_general(
        recv[1 - zh].reshape(HALF * 16, 128), basis_v[1 - zh], dims, preferred_element_type=F32
    )
    for e in range(2):
        for l in range(2):
            el = 2 * e + l
            out_ref[e, l] = total[el * 32 : el * 32 + 24] * factor[l]

    across.wait_send()
    left(zh)
    left(1 - zh)


def near_of(trees, k):
    return [s for s in range(MEMS) if k in trees[s][s]]


def body(gradient, perturbations, band_index, band_weight, wave_index, spectrum):
    trees = gather_trees()
    table = jnp.asarray(zonal_constant())
    basis = jnp.asarray(latitude_constant())
    place = jnp.asarray(spread_constant())
    hbm = pl.BlockSpec(memory_space=pl.ANY)
    dma = pltpu.SemaphoreType.DMA
    return pl.pallas_call(
        functools.partial(kernel, trees),
        name="alpha_adjoint",
        out_shape=jax.ShapeDtypeStruct((2, 2, 24, NDEG), F32),
        in_specs=[pl.BlockSpec(memory_space=pltpu.SMEM)] + [hbm] * 8,
        out_specs=pl.BlockSpec(memory_space=pltpu.VMEM),
        scratch_shapes=[
            pltpu.VMEM(gradient.shape, BF16),
            pltpu.VMEM(perturbations.shape, BF16),
            pltpu.VMEM(band_index.shape, jnp.int32),
            pltpu.VMEM(wave_index.shape, jnp.int32),
            pltpu.VMEM(spectrum.shape, F32),
            pltpu.VMEM(table.shape, BF16),
            pltpu.VMEM(basis.shape, BF16),
            pltpu.VMEM(place.shape, BF16),
            pltpu.VMEM((ROWS, 256), F32),
            pltpu.VMEM((2, ROWS, NLON), F32),
            pltpu.VMEM((24, NLON), F32),
            pltpu.VMEM((2, 24, NDEG), F32),
            pltpu.VMEM((MEMS, GROWS, 128), BF16),
            pltpu.VMEM((48, NLON), BF16),
            pltpu.VMEM((48, MT), BF16),
            pltpu.VMEM((48, MT), BF16),
            pltpu.VMEM((2, HALF, 16, 128), BF16),
            pltpu.VMEM((2, HALF, 16, 128), BF16),
            dma((9,)),
            dma((24,)),
            dma((MEMS,)),
            dma,
            dma,
            dma((2,)),
            dma((2,)),
        ],
        compiler_params=pltpu.CompilerParams(
            collective_id=0, has_side_effects=True, vmem_limit_bytes=40 * 2**20
        ),
    )(band_weight, gradient, perturbations, band_index, wave_index, spectrum, table, basis, place)


def solution(mesh):
    in_specs = (
        P(None, None, "space", "mem"),
        P("mem", None, None, "space", None),
        P("space", None),
        P(),
        P("space", None),
        P(),
    )
    out_specs = P("mem", None, "space", None)
    return jax.shard_map(body, mesh=mesh, in_specs=in_specs, out_specs=out_specs, check_vma=False)
```

```python
import functools
import math

import jax
import jax.numpy as jnp
import ml_dtypes
import numpy as np
from jax import lax
from jax.experimental import pallas as pl
from jax.experimental.pallas import tpu as pltpu
from jax.sharding import PartitionSpec as P

MESH = pl.DeviceIdType.MESH
BF16 = jnp.bfloat16
F32 = jnp.float32

MEMS = 8
HALF = 32
NLAT = 768
NLON = 1536
MT = 768
NDEG = 768
CYC = 12
FIELDS = 6
ROWS = 144
GROWS = 224

def gather_trees():
    trees = []
    for s in range(MEMS):
        tree = {n: [] for n in range(MEMS)}
        near = range(0, 4) if s < 4 else range(4, 8)
        relay = s + 4 if s < 4 else s - 4
        far = range(4, 8) if s < 4 else range(0, 4)
        tree[s] = [relay] + sorted((n for n in near if n != s), key=lambda n: -abs(n - s))
        tree[relay] = sorted((n for n in far if n != relay), key=lambda n: -abs(n - relay))
        trees.append(tree)
    return trees


def zonal_constant():
    phase = (np.arange(NLON)[:, None] * np.arange(MT)[None, :]) % NLON
    angle = phase * (2.0 * math.pi / NLON)
    pair = np.stack([np.cos(angle), -np.sin(angle)], axis=-1).reshape(NLON, 2 * MT)
    pair = (pair * math.sqrt(2.0 / NLON)).astype(np.float32).astype(ml_dtypes.bfloat16)
    return np.ascontiguousarray(pair.reshape(NLON, 2, MT).transpose(1, 0, 2))


def latitude_constant():
    phase = (np.arange(NDEG)[None, :] * (2 * np.arange(NLAT)[:, None] + 1)) % (4 * NLAT)
    basis = np.cos(phase * (math.pi / (2 * NLAT))) * math.sqrt(2.0 / NLAT)
    padded = np.zeros((2, HALF, 16, NDEG), np.float32)
    padded[:, :, :CYC] = basis.reshape(2, HALF, CYC, NDEG)
    return padded.reshape(2, HALF * 16, NDEG).astype(ml_dtypes.bfloat16)


def spread_constant():
    place = np.zeros((HALF * 24, HALF * 32), np.float32)
    for d in range(HALF):
        place[d * 24 + np.arange(24), d * 32 + np.arange(24)] = 1.0
    return place.astype(ml_dtypes.bfloat16)


def order_constant():
    order = np.zeros((64, 48), np.float32)
    for e in range(2):
        for l in range(2):
            for j in range(CYC):
                order[(2 * e + l) * 16 + j, e * 24 + 2 * j + l] = 1.0
    return order.astype(ml_dtypes.bfloat16)


def kernel(
    trees,
    weight_s, grad_h, pert_h, band_h, wave_h, spec_h, table_h, basis_h, place_h, order_v,
    out_ref,
    grad_v, pert_v, band_v, wave_v, spec_v, table_v, basis_v, place_v,
    gpack, area, factor, gbuf, alpha, zsend, zrecv, send, recv,
    load_sem, gs_sem, gr_sem, as_sem, ar_sem, bs_sem, br_sem,
):
    m = lax.axis_index("mem")
    space = lax.axis_index("space")
    zh = space // HALF
    s32 = space % HALF
    partner = (1 - zh) * HALF + s32

    loads = [
        (grad_h.reshape(ROWS, 192), grad_v), (pert_h.reshape(2, ROWS, NLON), pert_v), (band_h, band_v), (wave_h, wave_v), (spec_h, spec_v),
        (table_h.at[1 - zh], table_v.at[0]), (table_h.at[zh], table_v.at[1]), (place_h, place_v),
        (basis_h, basis_v),
    ]
    loads = [pltpu.make_async_copy(a, b, load_sem.at[i]) for i, (a, b) in enumerate(loads)]
    for c in loads:
        c.start()

    barrier = pltpu.get_barrier_semaphore()

    def greet(d, _):
        pl.semaphore_signal(barrier, inc=1, device_id=((m + d) % MEMS, space), device_id_type=MESH)
        return 0

    lax.fori_loop(1, MEMS, greet, 0)
    pl.semaphore_signal(barrier, inc=1, device_id=(m, partner), device_id_type=MESH)

    def greet_half(d, _):
        pl.semaphore_signal(
            barrier, inc=1, device_id=(m, zh * HALF + (s32 + d) % HALF), device_id_type=MESH
        )
        return 0

    lax.fori_loop(1, HALF, greet_half, 0)

    loads[0].wait()
    gpack[:, 0:192] = grad_v[...].astype(F32)
    lane = lax.broadcasted_iota(jnp.int32, (ROWS, 128), 1)
    low = lane < 64
    t0 = gpack[:, 0:128]
    t1 = gpack[:, 128:256]
    odd = m % 2
    full = jnp.where(odd == 1, jnp.where(low, pltpu.roll(t0, 64, 1), pltpu.roll(t1, 64, 1)), t0)
    part = jnp.where(odd == 1, t0, t1)
    turned = pltpu.roll(part, 64, 1)
    low72 = low[0:72]
    folded = jnp.where(
        odd == 1,
        jnp.where(low72, part[72:144], turned[0:72]),
        jnp.where(low72, part[0:72], turned[72:144]),
    )
    gbuf[m, 0:144] = full.astype(BF16)
    gbuf[m, 144:224] = jnp.concatenate([folded, jnp.zeros((8, 128), F32)], axis=0).astype(BF16)

    pl.semaphore_wait(barrier, MEMS - 1 + 1 + HALF - 1)

    def gather_copy(s, child, index):
        return pltpu.make_async_remote_copy(
            gbuf.at[s], gbuf.at[s], gs_sem.at[index], gr_sem.at[s],
            device_id=(child, space), device_id_type=MESH,
        )

    first = [[(k, c) for c in trees[k][k]] for k in range(MEMS)]
    later = []
    for k in range(MEMS):
        order = sorted((s for s in range(MEMS) if s != k), key=lambda s: (s not in near_of(trees, k), abs(s - k)))
        later.append(order)

    for k in range(MEMS):
        @pl.when(m == k)
        def _(k=k):
            for i, (s, c) in enumerate(first[k]):
                gather_copy(s, c, i).start()

    loads[2].wait()
    band = band_v[...]
    a = jnp.zeros((CYC, NLON), F32)
    for b in range(16):
        a = jnp.where(band == b, weight_s[b], a)
    for j in range(CYC):
        area[2 * j : 2 * j + 2] = jnp.broadcast_to(a[j : j + 1], (2, NLON))

    loads[3].wait()
    loads[4].wait()
    for t in range(6):
        idx = wave_v[:, t * 128 : t * 128 + 128]
        block = idx // 128
        place = idx % 128
        for l in range(2):
            got = jnp.zeros((CYC, 128), F32)
            for b in range(6):
                row = jnp.broadcast_to(spec_v[l : l + 1, b * 128 : b * 128 + 128], (CYC, 128))
                got = jnp.where(block == b, jnp.take_along_axis(row, place, axis=1), got)
            for r in range(CYC):
                factor[l, 2 * r : 2 * r + 2, t * 128 : t * 128 + 128] = jnp.broadcast_to(
                    got[r : r + 1], (2, 128)
                )

    for k in range(MEMS):
        @pl.when(m == k)
        def _(k=k):
            sent = list(first[k])
            for s in later[k]:
                gather_copy(s, 0, 0).wait_recv()
                for c in trees[s][k]:
                    gather_copy(s, c, len(sent)).start()
                    sent.append((s, c))
            for i, (s, c) in enumerate(sent):
                gather_copy(s, c, i).wait_send()

    loads[1].wait()
    low = low72
    for p in range(4):
        ge = gbuf[2 * p].astype(F32)
        go = gbuf[2 * p + 1].astype(F32)
        fe, fo = ge[144:216], go[144:216]
        mid = jnp.concatenate(
            [jnp.where(low, fe, fo), pltpu.roll(jnp.where(low, fo, fe), 64, 1)], axis=0
        )
        for t, tile in enumerate((ge[0:144], mid, go[0:144])):
            lanes = slice((3 * p + t) * 128, (3 * p + t) * 128 + 128)
            rows = []
            for e in range(2):
                pert = pert_v[e, :, lanes].astype(F32)
                acc = pert[0:24] * tile[0:24]
                for f in range(1, FIELDS):
                    acc = acc + pert[f * 24 : f * 24 + 24] * tile[f * 24 : f * 24 + 24]
                rows.append(area[:, lanes] * acc)
            alpha[:, lanes] = jnp.concatenate(rows, axis=0).astype(BF16)

    loads[5].wait()
    zsend[...] = jnp.dot(alpha[...], table_v[0], preferred_element_type=F32).astype(BF16)
    across = pltpu.make_async_remote_copy(
        zsend, zrecv, as_sem, ar_sem, device_id=(m, partner), device_id_type=MESH
    )
    across.start()
    loads[6].wait()
    mine = jnp.dot(alpha[...], table_v[1], preferred_element_type=F32).astype(BF16)

    lane = lax.broadcasted_iota(jnp.int32, (16, 128), 1)

    def message(zs, peer):
        return pltpu.make_async_remote_copy(
            send.at[zs, peer], recv.at[zs, s32], bs_sem.at[zs], br_sem.at[zs],
            device_id=(m, zh * HALF + peer), device_id_type=MESH,
        )

    def spread(z, zs):
        z = jnp.dot(order_v[...], z, preferred_element_type=F32).astype(BF16)
        y = jnp.dot(z, place_v[...], preferred_element_type=F32)
        for t in range(8):
            blocks = [y[16 * el : 16 * el + 16, t * 128 : t * 128 + 128] for el in range(4)]
            for d in range(4):
                whole = None
                for el in range(4):
                    shift = (32 * (el - d)) % 128
                    moved = pltpu.roll(blocks[el], shift, 1) if shift else blocks[el]
                    whole = moved if whole is None else jnp.where(lane >= 32 * el, moved, whole)
                send[zs, 4 * t + d] = whole.astype(BF16)
        recv[zs, s32] = send[zs, s32]

        def go(d, _):
            message(zs, (s32 + d) % HALF).start()
            return 0

        lax.fori_loop(1, HALF, go, 0)

    def arrived(zs):
        pltpu.make_async_copy(send.at[zs, 0:31], recv.at[zs, 0:31], br_sem.at[zs]).wait()

    def left(zs):
        pltpu.make_async_copy(send.at[zs, 0:31], recv.at[zs, 0:31], bs_sem.at[zs]).wait()

    loads[7].wait()
    spread(mine, zh)
    across.wait_recv()
    spread(zrecv[...], 1 - zh)

    loads[8].wait()
    arrived(zh)
    dims = (((0,), (0,)), ((), ()))
    total = lax.dot_general(
        recv[zh].reshape(HALF * 16, 128), basis_v[zh], dims, preferred_element_type=F32
    )
    arrived(1 - zh)
    total = total + lax.dot_general(
        recv[1 - zh].reshape(HALF * 16, 128), basis_v[1 - zh], dims, preferred_element_type=F32
    )
    for e in range(2):
        for l in range(2):
            el = 2 * e + l
            out_ref[e, l] = total[el * 32 : el * 32 + 24] * factor[l]

    across.wait_send()
    left(zh)
    left(1 - zh)


def near_of(trees, k):
    return [s for s in range(MEMS) if k in trees[s][s]]


def body(gradient, perturbations, band_index, band_weight, wave_index, spectrum):
    trees = gather_trees()
    table = jnp.asarray(zonal_constant())
    basis = jnp.asarray(latitude_constant())
    place = jnp.asarray(spread_constant())
    order = jnp.asarray(order_constant())
    gradient = gradient.transpose(0, 2, 1, 3)
    perturbations = perturbations.transpose(0, 1, 3, 2, 4)
    hbm = pl.BlockSpec(memory_space=pl.ANY)
    dma = pltpu.SemaphoreType.DMA
    return pl.pallas_call(
        functools.partial(kernel, trees),
        name="alpha_adjoint",
        out_shape=jax.ShapeDtypeStruct((2, 2, 24, NDEG), F32),
        in_specs=[pl.BlockSpec(memory_space=pltpu.SMEM)] + [hbm] * 8 + [pl.BlockSpec(memory_space=pltpu.VMEM)],
        out_specs=pl.BlockSpec(memory_space=pltpu.VMEM),
        scratch_shapes=[
            pltpu.VMEM((ROWS, 192), BF16),
            pltpu.VMEM((2, ROWS, NLON), BF16),
            pltpu.VMEM(band_index.shape, jnp.int32),
            pltpu.VMEM(wave_index.shape, jnp.int32),
            pltpu.VMEM(spectrum.shape, F32),
            pltpu.VMEM(table.shape, BF16),
            pltpu.VMEM(basis.shape, BF16),
            pltpu.VMEM(place.shape, BF16),
            pltpu.VMEM((ROWS, 256), F32),
            pltpu.VMEM((24, NLON), F32),
            pltpu.VMEM((2, 24, NDEG), F32),
            pltpu.VMEM((MEMS, GROWS, 128), BF16),
            pltpu.VMEM((48, NLON), BF16),
            pltpu.VMEM((48, MT), BF16),
            pltpu.VMEM((48, MT), BF16),
            pltpu.VMEM((2, HALF, 16, 128), BF16),
            pltpu.VMEM((2, HALF, 16, 128), BF16),
            dma((9,)),
            dma((24,)),
            dma((MEMS,)),
            dma,
            dma,
            dma((2,)),
            dma((2,)),
        ],
        compiler_params=pltpu.CompilerParams(
            collective_id=0, has_side_effects=True, vmem_limit_bytes=60 * 2**20
        ),
    )(band_weight, gradient, perturbations, band_index, wave_index, spectrum, table, basis, place, order)


def solution(mesh):
    in_specs = (
        P(None, None, "space", "mem"),
        P("mem", None, None, "space", None),
        P("space", None),
        P(),
        P("space", None),
        P(),
    )
    out_specs = P("mem", None, "space", None)
    return jax.shard_map(body, mesh=mesh, in_specs=in_specs, out_specs=out_specs, check_vma=False)
```

```python
import functools
import math

import jax
import jax.numpy as jnp
import ml_dtypes
import numpy as np
from jax import lax
from jax.experimental import pallas as pl
from jax.experimental.pallas import tpu as pltpu
from jax.sharding import PartitionSpec as P

MESH = pl.DeviceIdType.MESH
BF16 = jnp.bfloat16
F32 = jnp.float32

MEMS = 8
HALF = 32
NLAT = 768
NLON = 1536
MT = 768
NDEG = 768
CYC = 12
FIELDS = 6
ROWS = 144
GROWS = 224
REACH = 4
RING = 16

PARENTS = (
    (0, 0, 1, 4, 0, 3, 4, 4),
    (1, 1, 1, 1, 5, 2, 5, 5),
    (2, 0, 2, 2, 6, 6, 2, 6),
    (2, 0, 3, 3, 3, 7, 7, 3),
)


def gather_trees():
    parents = [list(p) for p in PARENTS]
    for s in reversed(range(4)):
        parents.append([7 - PARENTS[s][7 - n] for n in range(MEMS)])
    children = [
        [[c for c in range(MEMS) if c != s and parents[s][c] == n] for n in range(MEMS)] for s in range(MEMS)
    ]
    depths = []
    for s in range(MEMS):
        row = []
        for n in range(MEMS):
            depth = 0
            while n != s:
                assert abs(n - parents[s][n]) <= REACH
                n = parents[s][n]
                depth += 1
            row.append(depth)
        depths.append(row)
    for s in range(MEMS):
        for n in range(MEMS):
            children[s][n].sort(key=lambda c: (-len(children[s][c]), -abs(c - n)))
    return children, depths


def zonal_constant():
    phase = (np.arange(NLON)[:, None] * np.arange(MT)[None, :]) % NLON
    angle = phase * (2.0 * math.pi / NLON)
    pair = np.stack([np.cos(angle), -np.sin(angle)], axis=-1).reshape(NLON, 2 * MT)
    pair = (pair * math.sqrt(2.0 / NLON)).astype(np.float32).astype(ml_dtypes.bfloat16)
    return np.ascontiguousarray(pair.reshape(NLON, 2, MT).transpose(1, 0, 2))


def latitude_constant():
    phase = (np.arange(NDEG)[None, :] * (2 * np.arange(NLAT)[:, None] + 1)) % (4 * NLAT)
    basis = np.cos(phase * (math.pi / (2 * NLAT))) * math.sqrt(2.0 / NLAT)
    padded = np.zeros((2, HALF, 16, NDEG), np.float32)
    padded[:, :, :CYC] = basis.reshape(2, HALF, CYC, NDEG)
    return padded.reshape(2, HALF * 16, NDEG).astype(ml_dtypes.bfloat16)


def spread_constant():
    place = np.zeros((16 * 24, 16 * 32), np.float32)
    for d in range(16):
        place[d * 24 + np.arange(24), d * 32 + np.arange(24)] = 1.0
    return place.astype(ml_dtypes.bfloat16)


def order_constant():
    order = np.zeros((64, 48), np.float32)
    for e in range(2):
        for l in range(2):
            for j in range(CYC):
                order[(2 * e + l) * 16 + j, e * 24 + 2 * j + l] = 1.0
    return order.astype(ml_dtypes.bfloat16)


def kernel(
    trees,
    weight_s, grad_h, pert_h, band_h, wave_h, spec_h, table_h, basis_h, place_h, order_v,
    out_ref,
    grad_v, pert_v, band_v, wave_v, spec_v, table_v, basis_v, place_v,
    gpack, area, factor, gbuf, alpha, zsend, zrecv, send, recv,
    load_sem, gs_sem, gr_sem, as_sem, ar_sem, bs_sem, br_sem, ready,
):
    m = lax.axis_index("mem")
    space = lax.axis_index("space")
    zh = space // HALF
    s32 = space % HALF
    z = zh * MEMS + m

    def along(d, place=None):
        to = (z + d + RING) % RING
        return to % MEMS, to // MEMS * HALF + (s32 if place is None else place)

    loads = [
        (grad_h.reshape(ROWS, 192), grad_v), (band_h, band_v), (wave_h, wave_v), (spec_h, spec_v),
        (pert_h.reshape(2, ROWS, NLON), pert_v), (table_h.at[1 - zh], table_v.at[0]),
        (table_h.at[zh], table_v.at[1]), (place_h, place_v), (basis_h.at[zh], basis_v.at[0]),
        (basis_h.at[1 - zh], basis_v.at[1]),
    ]
    loads = [pltpu.make_async_copy(a, b, load_sem.at[i]) for i, (a, b) in enumerate(loads)]
    for c in loads:
        c.start()

    barrier = pltpu.get_barrier_semaphore()
    for d in (4, -4, 3, -3, 2, -2, 1, -1):
        pl.semaphore_signal(barrier, inc=1, device_id=along(d), device_id_type=MESH)

    def greet_half(d, _):
        pl.semaphore_signal(
            barrier, inc=1, device_id=(m, zh * HALF + (s32 + d) % HALF), device_id_type=MESH
        )
        return 0

    lax.fori_loop(1, HALF, greet_half, 0)

    loads[0].wait()
    gpack[:, 0:192] = grad_v[...].astype(F32)
    lane = lax.broadcasted_iota(jnp.int32, (ROWS, 128), 1)
    low = lane < 64
    t0 = gpack[:, 0:128]
    t1 = gpack[:, 128:256]
    odd = m % 2
    full = jnp.where(odd == 1, jnp.where(low, pltpu.roll(t0, 64, 1), pltpu.roll(t1, 64, 1)), t0)
    part = jnp.where(odd == 1, t0, t1)
    turned = pltpu.roll(part, 64, 1)
    low72 = low[0:72]
    folded = jnp.where(
        odd == 1,
        jnp.where(low72, part[72:144], turned[0:72]),
        jnp.where(low72, part[0:72], turned[72:144]),
    )
    gbuf[m, 0:144] = full.astype(BF16)
    gbuf[m, 144:224] = jnp.concatenate([folded, jnp.zeros((8, 128), F32)], axis=0).astype(BF16)

    pl.semaphore_wait(barrier, 2 * REACH + HALF - 1)

    def gather_copy(s, child, index):
        return pltpu.make_async_remote_copy(
            gbuf.at[s], gbuf.at[s], gs_sem.at[index], gr_sem.at[s],
            device_id=(child, space), device_id_type=MESH,
        )

    children, depths = trees
    for k in range(MEMS):
        @pl.when(m == k)
        def _(k=k):
            for i, c in enumerate(children[k][k]):
                gather_copy(k, c, i).start()

    for d in (4, -4, 1, -1):
        pl.semaphore_signal(ready, inc=1, device_id=along(d), device_id_type=MESH)

    loads[1].wait()
    band = band_v[...]
    a = jnp.zeros((CYC, NLON), F32)
    for b in range(16):
        a = jnp.where(band == b, weight_s[b], a)
    for j in range(CYC):
        area[2 * j : 2 * j + 2] = jnp.broadcast_to(a[j : j + 1], (2, NLON))

    loads[2].wait()
    loads[3].wait()
    for t in range(6):
        idx = wave_v[:, t * 128 : t * 128 + 128]
        block = idx // 128
        place = idx % 128
        for l in range(2):
            got = jnp.zeros((CYC, 128), F32)
            for b in range(6):
                row = jnp.broadcast_to(spec_v[l : l + 1, b * 128 : b * 128 + 128], (CYC, 128))
                got = jnp.where(block == b, jnp.take_along_axis(row, place, axis=1), got)
            for r in range(CYC):
                factor[l, 2 * r : 2 * r + 2, t * 128 : t * 128 + 128] = jnp.broadcast_to(
                    got[r : r + 1], (2, 128)
                )

    def passes(k):
        order = [s for s in range(MEMS) if s != k and children[s][k]]
        order.sort(key=lambda s: (depths[s][k], abs(s - k)))
        return order, [s for s in range(MEMS) if s != k and not children[s][k]]

    for k in range(MEMS):
        @pl.when(m == k)
        def _(k=k):
            count = len(children[k][k])
            through, last = passes(k)
            for s in through:
                gather_copy(s, 0, 0).wait_recv()
                for c in children[s][k]:
                    gather_copy(s, c, count).start()
                    count += 1
            for s in last:
                gather_copy(s, 0, 0).wait_recv()

    loads[4].wait()
    low = low72
    for p in range(4):
        ge = gbuf[2 * p].astype(F32)
        go = gbuf[2 * p + 1].astype(F32)
        fe, fo = ge[144:216], go[144:216]
        mid = jnp.concatenate(
            [jnp.where(low, fe, fo), pltpu.roll(jnp.where(low, fo, fe), 64, 1)], axis=0
        )
        for t, tile in enumerate((ge[0:144], mid, go[0:144])):
            lanes = slice((3 * p + t) * 128, (3 * p + t) * 128 + 128)
            rows = []
            for e in range(2):
                pert = pert_v[e, :, lanes].astype(F32)
                acc = pert[0:24] * tile[0:24]
                for f in range(1, FIELDS):
                    acc = acc + pert[f * 24 : f * 24 + 24] * tile[f * 24 : f * 24 + 24]
                rows.append(area[:, lanes] * acc)
            alpha[:, lanes] = jnp.concatenate(rows, axis=0).astype(BF16)

    pl.semaphore_wait(ready, 4)
    loads[5].wait()
    across = []
    for i, d in enumerate((7, -7)):
        part = jnp.dot(alpha[...], table_v[0, :, i * 384 : i * 384 + 384], preferred_element_type=F32)
        zsend[i] = part.astype(BF16)
        across.append(
            pltpu.make_async_remote_copy(
                zsend.at[i], zrecv.at[i], as_sem.at[i], ar_sem.at[i],
                device_id=along(d), device_id_type=MESH,
            )
        )
        across[i].start()
    loads[6].wait()
    mine = jnp.dot(alpha[...], table_v[1], preferred_element_type=F32).astype(BF16)

    lane = lax.broadcasted_iota(jnp.int32, (16, 128), 1)

    def message(kind, slot, to):
        return pltpu.make_async_remote_copy(
            send.at[kind, slot], recv.at[kind, s32], bs_sem.at[kind], br_sem.at[kind],
            device_id=to, device_id_type=MESH,
        )

    def spread(part, kind, base):
        part = jnp.dot(order_v[...], part, preferred_element_type=F32).astype(BF16)
        y = jnp.dot(part, place_v[...], preferred_element_type=F32)
        for t in range(4):
            blocks = [y[16 * el : 16 * el + 16, t * 128 : t * 128 + 128] for el in range(4)]
            for d in range(4):
                whole = None
                for el in range(4):
                    shift = (32 * (el - d)) % 128
                    moved = pltpu.roll(blocks[el], shift, 1) if shift else blocks[el]
                    whole = moved if whole is None else jnp.where(lane >= 32 * el, moved, whole)
                slot = base + 4 * t + d
                send[kind, slot] = whole.astype(BF16)
                if kind == 0:
                    @pl.when(s32 != slot)
                    def _(slot=slot):
                        message(0, slot, (m, zh * HALF + slot)).start()
                else:
                    message(1, slot, along(1 if base == 0 else -1, slot)).start()

    def arrived(kind, count):
        pltpu.make_async_copy(send.at[kind, 0:count], recv.at[kind, 0:count], br_sem.at[kind]).wait()

    def left(kind, count):
        pltpu.make_async_copy(send.at[kind, 0:count], recv.at[kind, 0:count], bs_sem.at[kind]).wait()

    loads[7].wait()
    spread(mine[:, 0:384], 0, 0)
    spread(mine[:, 384:768], 0, 16)
    recv[0, s32] = send[0, s32]
    for i in range(2):
        across[i].wait_recv()
        spread(zrecv[i], 1, 16 * i)

    loads[8].wait()
    arrived(0, HALF - 1)
    dims = (((0,), (0,)), ((), ()))
    total = lax.dot_general(
        recv[0].reshape(HALF * 16, 128), basis_v[0], dims, preferred_element_type=F32
    )
    loads[9].wait()
    arrived(1, HALF)
    total = total + lax.dot_general(
        recv[1].reshape(HALF * 16, 128), basis_v[1], dims, preferred_element_type=F32
    )
    for e in range(2):
        for l in range(2):
            el = 2 * e + l
            out_ref[e, l] = total[el * 32 : el * 32 + 24] * factor[l]

    for k in range(MEMS):
        @pl.when(m == k)
        def _(k=k):
            count = 0
            for s in [k] + passes(k)[0]:
                for c in children[s][k]:
                    gather_copy(s, c, count).wait_send()
                    count += 1
    for i in range(2):
        across[i].wait_send()
    left(0, HALF - 1)
    left(1, HALF)


def body(gradient, perturbations, band_index, band_weight, wave_index, spectrum):
    trees = gather_trees()
    table = jnp.asarray(zonal_constant())
    basis = jnp.asarray(latitude_constant())
    place = jnp.asarray(spread_constant())
    order = jnp.asarray(order_constant())
    gradient = gradient.transpose(0, 2, 1, 3)
    perturbations = perturbations.transpose(0, 1, 3, 2, 4)
    hbm = pl.BlockSpec(memory_space=pl.ANY)
    dma = pltpu.SemaphoreType.DMA
    return pl.pallas_call(
        functools.partial(kernel, trees),
        name="alpha_adjoint",
        out_shape=jax.ShapeDtypeStruct((2, 2, 24, NDEG), F32),
        in_specs=[pl.BlockSpec(memory_space=pltpu.SMEM)] + [hbm] * 8 + [pl.BlockSpec(memory_space=pltpu.VMEM)],
        out_specs=pl.BlockSpec(memory_space=pltpu.VMEM),
        scratch_shapes=[
            pltpu.VMEM((ROWS, 192), BF16),
            pltpu.VMEM((2, ROWS, NLON), BF16),
            pltpu.VMEM(band_index.shape, jnp.int32),
            pltpu.VMEM(wave_index.shape, jnp.int32),
            pltpu.VMEM(spectrum.shape, F32),
            pltpu.VMEM(table.shape, BF16),
            pltpu.VMEM(basis.shape, BF16),
            pltpu.VMEM(place.shape, BF16),
            pltpu.VMEM((ROWS, 256), F32),
            pltpu.VMEM((24, NLON), F32),
            pltpu.VMEM((2, 24, NDEG), F32),
            pltpu.VMEM((MEMS, GROWS, 128), BF16),
            pltpu.VMEM((48, NLON), BF16),
            pltpu.VMEM((2, 48, 384), BF16),
            pltpu.VMEM((2, 48, 384), BF16),
            pltpu.VMEM((2, HALF, 16, 128), BF16),
            pltpu.VMEM((2, HALF, 16, 128), BF16),
            dma((10,)),
            dma((24,)),
            dma((MEMS,)),
            dma((2,)),
            dma((2,)),
            dma((2,)),
            dma((2,)),
            pltpu.SemaphoreType.REGULAR,
        ],
        compiler_params=pltpu.CompilerParams(
            collective_id=0, has_side_effects=True, vmem_limit_bytes=60 * 2**20
        ),
    )(band_weight, gradient, perturbations, band_index, wave_index, spectrum, table, basis, place, order)


def solution(mesh):
    in_specs = (
        P(None, None, "space", "mem"),
        P("mem", None, None, "space", None),
        P("space", None),
        P(),
        P("space", None),
        P(),
    )
    out_specs = P("mem", None, "space", None)
    return jax.shard_map(body, mesh=mesh, in_specs=in_specs, out_specs=out_specs, check_vma=False)
```

```python
import functools
import math

import jax
import jax.numpy as jnp
import ml_dtypes
import numpy as np
from jax import lax
from jax.experimental import pallas as pl
from jax.experimental.pallas import tpu as pltpu
from jax.sharding import PartitionSpec as P

MESH = pl.DeviceIdType.MESH
BF16 = jnp.bfloat16
F32 = jnp.float32

MEMS = 8
HALF = 32
NLAT = 768
NLON = 1536
MT = 768
NDEG = 768
CYC = 12
FIELDS = 6
ROWS = 144
GROWS = 224
REACH = 4
RING = 16

PARENTS = (
    (0, 0, 0, 0, 0, 4, 4, 4),
    (1, 1, 1, 1, 5, 1, 5, 5),
    (2, 2, 2, 2, 6, 6, 2, 6),
    (3, 3, 3, 3, 7, 7, 7, 3),
    (4, 0, 0, 0, 4, 4, 4, 4),
    (1, 5, 1, 1, 5, 5, 5, 5),
    (2, 2, 6, 2, 6, 6, 6, 6),
    (3, 3, 3, 7, 7, 7, 7, 7),
)


def gather_trees():
    parents = PARENTS
    children = [
        [[c for c in range(MEMS) if c != s and parents[s][c] == n] for n in range(MEMS)] for s in range(MEMS)
    ]
    depths = []
    for s in range(MEMS):
        row = []
        for n in range(MEMS):
            depth = 0
            while n != s:
                assert abs(n - parents[s][n]) <= REACH
                n = parents[s][n]
                depth += 1
            row.append(depth)
        depths.append(row)
    for s in range(MEMS):
        for n in range(MEMS):
            children[s][n].sort(key=lambda c: (-len(children[s][c]), c))
    return children, depths


def zonal_constant():
    phase = (np.arange(NLON)[:, None] * np.arange(MT)[None, :]) % NLON
    angle = phase * (2.0 * math.pi / NLON)
    pair = np.stack([np.cos(angle), -np.sin(angle)], axis=-1).reshape(NLON, 2 * MT)
    pair = (pair * math.sqrt(2.0 / NLON)).astype(np.float32).astype(ml_dtypes.bfloat16)
    return np.ascontiguousarray(pair.reshape(NLON, 2, MT).transpose(1, 0, 2))


def latitude_constant():
    phase = (np.arange(NDEG)[None, :] * (2 * np.arange(NLAT)[:, None] + 1)) % (4 * NLAT)
    basis = np.cos(phase * (math.pi / (2 * NLAT))) * math.sqrt(2.0 / NLAT)
    padded = np.zeros((2, HALF, 16, NDEG), np.float32)
    padded[:, :, :CYC] = basis.reshape(2, HALF, CYC, NDEG)
    return padded.reshape(2, HALF * 16, NDEG).astype(ml_dtypes.bfloat16)


def spread_constant():
    place = np.zeros((16 * 24, 16 * 32), np.float32)
    for d in range(16):
        place[d * 24 + np.arange(24), d * 32 + np.arange(24)] = 1.0
    return place.astype(ml_dtypes.bfloat16)


def order_constant():
    order = np.zeros((64, 48), np.float32)
    for e in range(2):
        for l in range(2):
            for j in range(CYC):
                order[(2 * e + l) * 16 + j, e * 24 + 2 * j + l] = 1.0
    return order.astype(ml_dtypes.bfloat16)


def kernel(
    trees,
    weight_s, grad_h, pert_h, band_h, wave_h, spec_h, table_h, basis_h, place_h, order_v,
    out_ref,
    grad_v, pert_v, band_v, wave_v, spec_v, table_v, basis_v, place_v,
    gpack, area, factor, gbuf, alpha, zsend, zrecv, send, recv,
    load_sem, gs_sem, gr_sem, as_sem, ar_sem, bs_sem, br_sem, ready,
):
    m = lax.axis_index("mem")
    space = lax.axis_index("space")
    zh = space // HALF
    s32 = space % HALF
    z = zh * MEMS + m

    def along(d, place=None):
        to = (z + d + RING) % RING
        return to % MEMS, to // MEMS * HALF + (s32 if place is None else place)

    loads = [
        (grad_h.reshape(ROWS, 192), grad_v), (band_h, band_v), (wave_h, wave_v), (spec_h, spec_v),
        (pert_h.reshape(2, ROWS, NLON), pert_v), (table_h.at[1 - zh], table_v.at[0]),
        (table_h.at[zh], table_v.at[1]), (place_h, place_v), (basis_h.at[zh], basis_v.at[0]),
        (basis_h.at[1 - zh], basis_v.at[1]),
    ]
    loads = [pltpu.make_async_copy(a, b, load_sem.at[i]) for i, (a, b) in enumerate(loads)]
    for c in loads:
        c.start()

    barrier = pltpu.get_barrier_semaphore()
    for d in (4, -4, 3, -3, 2, -2, 1, -1):
        pl.semaphore_signal(barrier, inc=1, device_id=along(d), device_id_type=MESH)

    def greet_half(d, _):
        pl.semaphore_signal(
            barrier, inc=1, device_id=(m, zh * HALF + (s32 + d) % HALF), device_id_type=MESH
        )
        return 0

    lax.fori_loop(1, HALF, greet_half, 0)

    loads[0].wait()
    gpack[:, 0:192] = grad_v[...].astype(F32)
    lane = lax.broadcasted_iota(jnp.int32, (ROWS, 128), 1)
    low = lane < 64
    t0 = gpack[:, 0:128]
    t1 = gpack[:, 128:256]
    odd = m % 2
    full = jnp.where(odd == 1, jnp.where(low, pltpu.roll(t0, 64, 1), pltpu.roll(t1, 64, 1)), t0)
    part = jnp.where(odd == 1, t0, t1)
    turned = pltpu.roll(part, 64, 1)
    low72 = low[0:72]
    folded = jnp.where(
        odd == 1,
        jnp.where(low72, part[72:144], turned[0:72]),
        jnp.where(low72, part[0:72], turned[72:144]),
    )
    gbuf[m, 0:144] = full.astype(BF16)
    gbuf[m, 144:224] = jnp.concatenate([folded, jnp.zeros((8, 128), F32)], axis=0).astype(BF16)

    pl.semaphore_wait(barrier, 2 * REACH + HALF - 1)

    def gather_copy(s, child, index):
        return pltpu.make_async_remote_copy(
            gbuf.at[s], gbuf.at[s], gs_sem.at[index], gr_sem.at[s],
            device_id=(child, space), device_id_type=MESH,
        )

    children, depths = trees
    for k in range(MEMS):
        @pl.when(m == k)
        def _(k=k):
            for i, c in enumerate(children[k][k]):
                gather_copy(k, c, i).start()

    for d in (4, -4, 1, -1):
        pl.semaphore_signal(ready, inc=1, device_id=along(d), device_id_type=MESH)

    loads[1].wait()
    band = band_v[...]
    a = jnp.zeros((CYC, NLON), F32)
    for b in range(16):
        a = jnp.where(band == b, weight_s[b], a)
    for j in range(CYC):
        area[2 * j : 2 * j + 2] = jnp.broadcast_to(a[j : j + 1], (2, NLON))

    loads[2].wait()
    loads[3].wait()
    for t in range(6):
        idx = wave_v[:, t * 128 : t * 128 + 128]
        block = idx // 128
        place = idx % 128
        for l in range(2):
            got = jnp.zeros((CYC, 128), F32)
            for b in range(6):
                row = jnp.broadcast_to(spec_v[l : l + 1, b * 128 : b * 128 + 128], (CYC, 128))
                got = jnp.where(block == b, jnp.take_along_axis(row, place, axis=1), got)
            for r in range(CYC):
                factor[l, 2 * r : 2 * r + 2, t * 128 : t * 128 + 128] = jnp.broadcast_to(
                    got[r : r + 1], (2, 128)
                )

    def passes(k):
        order = [s for s in range(MEMS) if s != k and children[s][k]]
        order.sort(key=lambda s: (depths[s][k], abs(s - k)))
        return order, [s for s in range(MEMS) if s != k and not children[s][k]]

    for k in range(MEMS):
        @pl.when(m == k)
        def _(k=k):
            count = len(children[k][k])
            through, last = passes(k)
            for s in through:
                gather_copy(s, 0, 0).wait_recv()
                for c in children[s][k]:
                    gather_copy(s, c, count).start()
                    count += 1
            for s in last:
                gather_copy(s, 0, 0).wait_recv()

    loads[4].wait()
    low = low72
    for p in range(4):
        ge = gbuf[2 * p].astype(F32)
        go = gbuf[2 * p + 1].astype(F32)
        fe, fo = ge[144:216], go[144:216]
        mid = jnp.concatenate(
            [jnp.where(low, fe, fo), pltpu.roll(jnp.where(low, fo, fe), 64, 1)], axis=0
        )
        for t, tile in enumerate((ge[0:144], mid, go[0:144])):
            lanes = slice((3 * p + t) * 128, (3 * p + t) * 128 + 128)
            rows = []
            for e in range(2):
                pert = pert_v[e, :, lanes].astype(F32)
                acc = pert[0:24] * tile[0:24]
                for f in range(1, FIELDS):
                    acc = acc + pert[f * 24 : f * 24 + 24] * tile[f * 24 : f * 24 + 24]
                rows.append(area[:, lanes] * acc)
            alpha[:, lanes] = jnp.concatenate(rows, axis=0).astype(BF16)

    pl.semaphore_wait(ready, 4)
    across = [
        pltpu.make_async_remote_copy(
            zsend.at[i], zrecv.at[i], as_sem.at[i], ar_sem.at[i],
            device_id=along(d), device_id_type=MESH,
        )
        for i, d in enumerate((7, -7))
    ]
    for i in range(5, 10):
        loads[i].wait()

    def cross_over():
        for i in range(2):
            part = jnp.dot(
                alpha[...], table_v[0, :, i * 384 : i * 384 + 384], preferred_element_type=F32
            )
            zsend[i] = part.astype(BF16)
            across[i].start()

    lane = lax.broadcasted_iota(jnp.int32, (16, 128), 1)

    def message(kind, slot, to):
        return pltpu.make_async_remote_copy(
            send.at[kind, slot], recv.at[kind, s32], bs_sem.at[kind], br_sem.at[kind],
            device_id=to, device_id_type=MESH,
        )

    def spread(part, kind, base):
        part = jnp.dot(order_v[...], part, preferred_element_type=F32).astype(BF16)
        y = jnp.dot(part, place_v[...], preferred_element_type=F32)
        for t in range(4):
            blocks = [y[16 * el : 16 * el + 16, t * 128 : t * 128 + 128] for el in range(4)]
            for d in range(4):
                whole = None
                for el in range(4):
                    shift = (32 * (el - d)) % 128
                    moved = pltpu.roll(blocks[el], shift, 1) if shift else blocks[el]
                    whole = moved if whole is None else jnp.where(lane >= 32 * el, moved, whole)
                slot = base + 4 * t + d
                send[kind, slot] = whole.astype(BF16)
                if kind == 0:
                    @pl.when(s32 != slot)
                    def _(slot=slot):
                        message(0, slot, (m, zh * HALF + slot)).start()
                else:
                    message(1, slot, along(1 if base == 0 else -1, slot)).start()

    def arrived(kind, count):
        pltpu.make_async_copy(send.at[kind, 0:count], recv.at[kind, 0:count], br_sem.at[kind]).wait()

    def left(kind, count):
        pltpu.make_async_copy(send.at[kind, 0:count], recv.at[kind, 0:count], bs_sem.at[kind]).wait()

    def keep():
        mine = jnp.dot(alpha[...], table_v[1], preferred_element_type=F32).astype(BF16)
        spread(mine[:, 0:384], 0, 0)
        spread(mine[:, 384:768], 0, 16)
        recv[0, s32] = send[0, s32]

    early = zh == 1
    pl.when(early)(cross_over)
    keep()
    pl.when(jnp.logical_not(early))(cross_over)
    for i in range(2):
        across[i].wait_recv()
        spread(zrecv[i], 1, 16 * i)

    arrived(0, HALF - 1)
    dims = (((0,), (0,)), ((), ()))
    total = lax.dot_general(
        recv[0].reshape(HALF * 16, 128), basis_v[0], dims, preferred_element_type=F32
    )
    arrived(1, HALF)
    total = total + lax.dot_general(
        recv[1].reshape(HALF * 16, 128), basis_v[1], dims, preferred_element_type=F32
    )
    for e in range(2):
        for l in range(2):
            el = 2 * e + l
            out_ref[e, l] = total[el * 32 : el * 32 + 24] * factor[l]

    for k in range(MEMS):
        @pl.when(m == k)
        def _(k=k):
            count = 0
            for s in [k] + passes(k)[0]:
                for c in children[s][k]:
                    gather_copy(s, c, count).wait_send()
                    count += 1
    for i in range(2):
        across[i].wait_send()
    left(0, HALF - 1)
    left(1, HALF)


def body(gradient, perturbations, band_index, band_weight, wave_index, spectrum):
    trees = gather_trees()
    table = jnp.asarray(zonal_constant())
    basis = jnp.asarray(latitude_constant())
    place = jnp.asarray(spread_constant())
    order = jnp.asarray(order_constant())
    gradient = gradient.transpose(0, 2, 1, 3)
    perturbations = perturbations.transpose(0, 1, 3, 2, 4)
    hbm = pl.BlockSpec(memory_space=pl.ANY)
    dma = pltpu.SemaphoreType.DMA
    return pl.pallas_call(
        functools.partial(kernel, trees),
        name="alpha_adjoint",
        out_shape=pltpu.VMEM((2, 2, 24, NDEG), F32),
        in_specs=[pl.BlockSpec(memory_space=pltpu.SMEM)] + [hbm] * 8 + [pl.BlockSpec(memory_space=pltpu.VMEM)],
        out_specs=pl.BlockSpec(memory_space=pltpu.VMEM),
        scratch_shapes=[
            pltpu.VMEM((ROWS, 192), BF16),
            pltpu.VMEM((2, ROWS, NLON), BF16),
            pltpu.VMEM(band_index.shape, jnp.int32),
            pltpu.VMEM(wave_index.shape, jnp.int32),
            pltpu.VMEM(spectrum.shape, F32),
            pltpu.VMEM(table.shape, BF16),
            pltpu.VMEM(basis.shape, BF16),
            pltpu.VMEM(place.shape, BF16),
            pltpu.VMEM((ROWS, 256), F32),
            pltpu.VMEM((24, NLON), F32),
            pltpu.VMEM((2, 24, NDEG), F32),
            pltpu.VMEM((MEMS, GROWS, 128), BF16),
            pltpu.VMEM((48, NLON), BF16),
            pltpu.VMEM((2, 48, 384), BF16),
            pltpu.VMEM((2, 48, 384), BF16),
            pltpu.VMEM((2, HALF, 16, 128), BF16),
            pltpu.VMEM((2, HALF, 16, 128), BF16),
            dma((10,)),
            dma((24,)),
            dma((MEMS,)),
            dma((2,)),
            dma((2,)),
            dma((2,)),
            dma((2,)),
            pltpu.SemaphoreType.REGULAR,
        ],
        compiler_params=pltpu.CompilerParams(
            collective_id=0, has_side_effects=True, vmem_limit_bytes=60 * 2**20
        ),
    )(band_weight, gradient, perturbations, band_index, wave_index, spectrum, table, basis, place, order)


def solution(mesh):
    in_specs = (
        P(None, None, "space", "mem"),
        P("mem", None, None, "space", None),
        P("space", None),
        P(),
        P("space", None),
        P(),
    )
    out_specs = P("mem", None, "space", None)
    return jax.shard_map(body, mesh=mesh, in_specs=in_specs, out_specs=out_specs, check_vma=False)
```

```python
import functools
import math

import jax
import jax.numpy as jnp
import ml_dtypes
import numpy as np
from jax import lax
from jax.experimental import pallas as pl
from jax.experimental.pallas import tpu as pltpu
from jax.sharding import PartitionSpec as P

MESH = pl.DeviceIdType.MESH
BF16 = jnp.bfloat16
F32 = jnp.float32

MEMS = 8
HALF = 32
NLAT = 768
NLON = 1536
MT = 768
NDEG = 768
CYC = 12
FIELDS = 6
ROWS = 144
GROWS = 224
REACH = 4
RING = 16

PARENTS = (
    (0, 0, 0, 0, 0, 4, 4, 4),
    (1, 1, 1, 1, 5, 1, 5, 5),
    (2, 2, 2, 2, 6, 6, 2, 6),
    (3, 3, 3, 3, 7, 7, 7, 3),
    (4, 0, 0, 0, 4, 4, 4, 4),
    (1, 5, 1, 1, 5, 5, 5, 5),
    (2, 2, 6, 2, 6, 6, 6, 6),
    (3, 3, 3, 7, 7, 7, 7, 7),
)


def gather_trees():
    parents = PARENTS
    children = [
        [[c for c in range(MEMS) if c != s and parents[s][c] == n] for n in range(MEMS)] for s in range(MEMS)
    ]
    depths = []
    for s in range(MEMS):
        row = []
        for n in range(MEMS):
            depth = 0
            while n != s:
                assert abs(n - parents[s][n]) <= REACH
                n = parents[s][n]
                depth += 1
            row.append(depth)
        depths.append(row)
    for s in range(MEMS):
        for n in range(MEMS):
            children[s][n].sort(key=lambda c: (-len(children[s][c]), c))
    return children, depths


def zonal_constant():
    phase = (np.arange(NLON)[:, None] * np.arange(MT)[None, :]) % NLON
    angle = phase * (2.0 * math.pi / NLON)
    pair = np.stack([np.cos(angle), -np.sin(angle)], axis=-1).reshape(NLON, 2 * MT)
    pair = (pair * math.sqrt(2.0 / NLON)).astype(np.float32).astype(ml_dtypes.bfloat16)
    return np.ascontiguousarray(pair.reshape(NLON, 2, MT).transpose(1, 0, 2))


def latitude_constant():
    phase = (np.arange(NDEG)[None, :] * (2 * np.arange(NLAT)[:, None] + 1)) % (4 * NLAT)
    basis = np.cos(phase * (math.pi / (2 * NLAT))) * math.sqrt(2.0 / NLAT)
    padded = np.zeros((2, HALF, 16, NDEG), np.float32)
    padded[:, :, :CYC] = basis.reshape(2, HALF, CYC, NDEG)
    return padded.reshape(2, HALF * 16, NDEG).astype(ml_dtypes.bfloat16)


def spread_constant():
    place = np.zeros((16 * 24, 16 * 32), np.float32)
    for d in range(16):
        place[d * 24 + np.arange(24), d * 32 + np.arange(24)] = 1.0
    return place.astype(ml_dtypes.bfloat16)


def order_constant():
    order = np.zeros((64, 48), np.float32)
    for e in range(2):
        for l in range(2):
            for j in range(CYC):
                order[(2 * e + l) * 16 + j, e * 24 + 2 * j + l] = 1.0
    return order.astype(ml_dtypes.bfloat16)


def kernel(
    trees,
    weight_h, grad_h, pert_h, band_h, wave_h, spec_h, table_h, basis_h, place_h, order_h,
    out_ref,
    weight_s, grad_v, pert_v, band_v, wave_v, spec_v, table_v, basis_v, place_v, order_v,
    gpack, area, factor, gbuf, alpha, zsend, zrecv, send, recv,
    load_sem, gs_sem, gr_sem, as_sem, ar_sem, bs_sem, br_sem, ready,
):
    m = lax.axis_index("mem")
    space = lax.axis_index("space")
    zh = space // HALF
    s32 = space % HALF
    z = zh * MEMS + m

    def along(d, place=None):
        to = (z + d + RING) % RING
        return to % MEMS, to // MEMS * HALF + (s32 if place is None else place)

    loads = [
        (grad_h.reshape(ROWS, 192), grad_v), (band_h, band_v), (wave_h, wave_v), (spec_h, spec_v),
        (pert_h.reshape(2, ROWS, NLON), pert_v), (table_h.at[1 - zh], table_v.at[0]),
        (table_h.at[zh], table_v.at[1]), (place_h, place_v), (basis_h.at[zh], basis_v.at[0]),
        (basis_h.at[1 - zh], basis_v.at[1]), (order_h, order_v), (weight_h, weight_s),
    ]
    loads = [pltpu.make_async_copy(a, b, load_sem.at[i]) for i, (a, b) in enumerate(loads)]
    loads[0].start()

    barrier = pltpu.get_barrier_semaphore()
    for d in (4, -4, 3, -3, 2, -2, 1, -1):
        pl.semaphore_signal(barrier, inc=1, device_id=along(d), device_id_type=MESH)

    def greet_half(d, _):
        pl.semaphore_signal(
            barrier, inc=1, device_id=(m, zh * HALF + (s32 + d) % HALF), device_id_type=MESH
        )
        return 0

    lax.fori_loop(1, HALF, greet_half, 0)
    for c in [loads[11]] + loads[1:11]:
        c.start()

    loads[0].wait()
    gpack[:, 0:192] = grad_v[...].astype(F32)
    lane = lax.broadcasted_iota(jnp.int32, (ROWS, 128), 1)
    low = lane < 64
    t0 = gpack[:, 0:128]
    t1 = gpack[:, 128:256]
    odd = m % 2
    full = jnp.where(odd == 1, jnp.where(low, pltpu.roll(t0, 64, 1), pltpu.roll(t1, 64, 1)), t0)
    part = jnp.where(odd == 1, t0, t1)
    turned = pltpu.roll(part, 64, 1)
    low72 = low[0:72]
    folded = jnp.where(
        odd == 1,
        jnp.where(low72, part[72:144], turned[0:72]),
        jnp.where(low72, part[0:72], turned[72:144]),
    )
    gbuf[m, 0:144] = full.astype(BF16)
    gbuf[m, 144:224] = jnp.concatenate([folded, jnp.zeros((8, 128), F32)], axis=0).astype(BF16)

    pl.semaphore_wait(barrier, 2 * REACH + HALF - 1)

    def gather_copy(s, child, index):
        return pltpu.make_async_remote_copy(
            gbuf.at[s], gbuf.at[s], gs_sem.at[index], gr_sem.at[s],
            device_id=(child, space), device_id_type=MESH,
        )

    children, depths = trees
    for k in range(MEMS):
        @pl.when(m == k)
        def _(k=k):
            for i, c in enumerate(children[k][k]):
                gather_copy(k, c, i).start()

    for d in (4, -4, 1, -1):
        pl.semaphore_signal(ready, inc=1, device_id=along(d), device_id_type=MESH)

    loads[1].wait()
    loads[11].wait()
    band = band_v[...]
    a = jnp.zeros((CYC, NLON), F32)
    for b in range(16):
        a = jnp.where(band == b, weight_s[b], a)
    for j in range(CYC):
        area[2 * j : 2 * j + 2] = jnp.broadcast_to(a[j : j + 1], (2, NLON))

    loads[2].wait()
    loads[3].wait()
    for t in range(6):
        idx = wave_v[:, t * 128 : t * 128 + 128]
        block = idx // 128
        place = idx % 128
        for l in range(2):
            got = jnp.zeros((CYC, 128), F32)
            for b in range(6):
                row = jnp.broadcast_to(spec_v[l : l + 1, b * 128 : b * 128 + 128], (CYC, 128))
                got = jnp.where(block == b, jnp.take_along_axis(row, place, axis=1), got)
            for r in range(CYC):
                factor[l, 2 * r : 2 * r + 2, t * 128 : t * 128 + 128] = jnp.broadcast_to(
                    got[r : r + 1], (2, 128)
                )

    def passes(k):
        order = [s for s in range(MEMS) if s != k and children[s][k]]
        order.sort(key=lambda s: (depths[s][k], abs(s - k)))
        return order, [s for s in range(MEMS) if s != k and not children[s][k]]

    for k in range(MEMS):
        @pl.when(m == k)
        def _(k=k):
            count = len(children[k][k])
            through, last = passes(k)
            for s in through:
                gather_copy(s, 0, 0).wait_recv()
                for c in children[s][k]:
                    gather_copy(s, c, count).start()
                    count += 1
            for s in last:
                gather_copy(s, 0, 0).wait_recv()

    loads[4].wait()
    low = low72
    for p in range(4):
        ge = gbuf[2 * p].astype(F32)
        go = gbuf[2 * p + 1].astype(F32)
        fe, fo = ge[144:216], go[144:216]
        mid = jnp.concatenate(
            [jnp.where(low, fe, fo), pltpu.roll(jnp.where(low, fo, fe), 64, 1)], axis=0
        )
        for t, tile in enumerate((ge[0:144], mid, go[0:144])):
            lanes = slice((3 * p + t) * 128, (3 * p + t) * 128 + 128)
            rows = []
            for e in range(2):
                pert = pert_v[e, :, lanes].astype(F32)
                acc = pert[0:24] * tile[0:24]
                for f in range(1, FIELDS):
                    acc = acc + pert[f * 24 : f * 24 + 24] * tile[f * 24 : f * 24 + 24]
                rows.append(area[:, lanes] * acc)
            alpha[:, lanes] = jnp.concatenate(rows, axis=0).astype(BF16)

    pl.semaphore_wait(ready, 4)
    across = [
        pltpu.make_async_remote_copy(
            zsend.at[i], zrecv.at[i], as_sem.at[i], ar_sem.at[i],
            device_id=along(d), device_id_type=MESH,
        )
        for i, d in enumerate((7, -7))
    ]
    for i in range(5, 11):
        loads[i].wait()

    def cross_over():
        for i in range(2):
            part = jnp.dot(
                alpha[...], table_v[0, :, i * 384 : i * 384 + 384], preferred_element_type=F32
            )
            zsend[i] = part.astype(BF16)
            across[i].start()

    lane = lax.broadcasted_iota(jnp.int32, (16, 128), 1)

    def message(kind, slot, to):
        return pltpu.make_async_remote_copy(
            send.at[kind, slot], recv.at[kind, s32], bs_sem.at[kind], br_sem.at[kind],
            device_id=to, device_id_type=MESH,
        )

    def spread(part, kind, base):
        part = jnp.dot(order_v[...], part, preferred_element_type=F32).astype(BF16)
        y = jnp.dot(part, place_v[...], preferred_element_type=F32)
        for t in range(4):
            blocks = [y[16 * el : 16 * el + 16, t * 128 : t * 128 + 128] for el in range(4)]
            for d in range(4):
                whole = None
                for el in range(4):
                    shift = (32 * (el - d)) % 128
                    moved = pltpu.roll(blocks[el], shift, 1) if shift else blocks[el]
                    whole = moved if whole is None else jnp.where(lane >= 32 * el, moved, whole)
                slot = base + 4 * t + d
                send[kind, slot] = whole.astype(BF16)
                if kind == 0:
                    @pl.when(s32 != slot)
                    def _(slot=slot):
                        message(0, slot, (m, zh * HALF + slot)).start()
                else:
                    message(1, slot, along(1 if base == 0 else -1, slot)).start()

    def arrived(kind, count):
        pltpu.make_async_copy(send.at[kind, 0:count], recv.at[kind, 0:count], br_sem.at[kind]).wait()

    def left(kind, count):
        pltpu.make_async_copy(send.at[kind, 0:count], recv.at[kind, 0:count], bs_sem.at[kind]).wait()

    def keep():
        mine = jnp.dot(alpha[...], table_v[1], preferred_element_type=F32).astype(BF16)
        spread(mine[:, 0:384], 0, 0)
        spread(mine[:, 384:768], 0, 16)
        recv[0, s32] = send[0, s32]

    early = zh == 1
    pl.when(early)(cross_over)
    keep()
    pl.when(jnp.logical_not(early))(cross_over)
    for i in range(2):
        across[i].wait_recv()
        spread(zrecv[i], 1, 16 * i)

    arrived(0, HALF - 1)
    dims = (((0,), (0,)), ((), ()))
    total = lax.dot_general(
        recv[0].reshape(HALF * 16, 128), basis_v[0], dims, preferred_element_type=F32
    )
    arrived(1, HALF)
    total = total + lax.dot_general(
        recv[1].reshape(HALF * 16, 128), basis_v[1], dims, preferred_element_type=F32
    )
    for e in range(2):
        for l in range(2):
            el = 2 * e + l
            out_ref[e, l] = total[el * 32 : el * 32 + 24] * factor[l]

    for k in range(MEMS):
        @pl.when(m == k)
        def _(k=k):
            count = 0
            for s in [k] + passes(k)[0]:
                for c in children[s][k]:
                    gather_copy(s, c, count).wait_send()
                    count += 1
    for i in range(2):
        across[i].wait_send()
    left(0, HALF - 1)
    left(1, HALF)


def body(gradient, perturbations, band_index, band_weight, wave_index, spectrum):
    trees = gather_trees()
    table = jnp.asarray(zonal_constant())
    basis = jnp.asarray(latitude_constant())
    place = jnp.asarray(spread_constant())
    order = jnp.asarray(order_constant())
    gradient = gradient.transpose(0, 2, 1, 3)
    perturbations = perturbations.transpose(0, 1, 3, 2, 4)
    hbm = pl.BlockSpec(memory_space=pl.ANY)
    dma = pltpu.SemaphoreType.DMA
    return pl.pallas_call(
        functools.partial(kernel, trees),
        name="alpha_adjoint",
        out_shape=pltpu.VMEM((2, 2, 24, NDEG), F32),
        in_specs=[hbm] * 10,
        out_specs=pl.BlockSpec(memory_space=pltpu.VMEM),
        scratch_shapes=[
            pltpu.SMEM(band_weight.shape, F32),
            pltpu.VMEM((ROWS, 192), BF16),
            pltpu.VMEM((2, ROWS, NLON), BF16),
            pltpu.VMEM(band_index.shape, jnp.int32),
            pltpu.VMEM(wave_index.shape, jnp.int32),
            pltpu.VMEM(spectrum.shape, F32),
            pltpu.VMEM(table.shape, BF16),
            pltpu.VMEM(basis.shape, BF16),
            pltpu.VMEM(place.shape, BF16),
            pltpu.VMEM(order.shape, BF16),
            pltpu.VMEM((ROWS, 256), F32),
            pltpu.VMEM((24, NLON), F32),
            pltpu.VMEM((2, 24, NDEG), F32),
            pltpu.VMEM((MEMS, GROWS, 128), BF16),
            pltpu.VMEM((48, NLON), BF16),
            pltpu.VMEM((2, 48, 384), BF16),
            pltpu.VMEM((2, 48, 384), BF16),
            pltpu.VMEM((2, HALF, 16, 128), BF16),
            pltpu.VMEM((2, HALF, 16, 128), BF16),
            dma((12,)),
            dma((24,)),
            dma((MEMS,)),
            dma((2,)),
            dma((2,)),
            dma((2,)),
            dma((2,)),
            pltpu.SemaphoreType.REGULAR,
        ],
        compiler_params=pltpu.CompilerParams(
            collective_id=0, has_side_effects=True, vmem_limit_bytes=60 * 2**20
        ),
    )(band_weight, gradient, perturbations, band_index, wave_index, spectrum, table, basis, place, order)


def solution(mesh):
    in_specs = (
        P(None, None, "space", "mem"),
        P("mem", None, None, "space", None),
        P("space", None),
        P(),
        P("space", None),
        P(),
    )
    out_specs = P("mem", None, "space", None)
    return jax.shard_map(body, mesh=mesh, in_specs=in_specs, out_specs=out_specs, check_vma=False)
```

```python
import functools
import math

import jax
import jax.numpy as jnp
import ml_dtypes
import numpy as np
from jax import lax
from jax.experimental import pallas as pl
from jax.experimental.pallas import tpu as pltpu
from jax.sharding import PartitionSpec as P

MESH = pl.DeviceIdType.MESH
BF16 = jnp.bfloat16
F32 = jnp.float32

MEMS = 8
HALF = 32
NLAT = 768
NLON = 1536
MT = 768
NDEG = 768
CYC = 12
FIELDS = 6
ROWS = 144
GROWS = 224
REACH = 4
RING = 16

PARENTS = (
    (0, 0, 0, 2, 0, 4, 4, 6),
    (1, 1, 1, 2, 5, 1, 5, 6),
    (1, 2, 2, 2, 5, 6, 2, 6),
    (1, 3, 3, 3, 5, 7, 7, 3),
    (4, 0, 0, 2, 4, 4, 4, 6),
    (1, 5, 1, 2, 5, 5, 5, 6),
    (1, 2, 6, 2, 5, 6, 6, 6),
    (1, 3, 3, 7, 5, 7, 7, 7),
)


def gather_trees():
    parents = PARENTS
    children = [
        [[c for c in range(MEMS) if c != s and parents[s][c] == n] for n in range(MEMS)] for s in range(MEMS)
    ]
    depths = []
    for s in range(MEMS):
        row = []
        for n in range(MEMS):
            depth = 0
            while n != s:
                assert abs(n - parents[s][n]) <= REACH
                n = parents[s][n]
                depth += 1
            row.append(depth)
        depths.append(row)
    for s in range(MEMS):
        for n in range(MEMS):
            children[s][n].sort(key=lambda c: (-len(children[s][c]), c))
    return children, depths


def zonal_constant():
    phase = (np.arange(NLON)[:, None] * np.arange(MT)[None, :]) % NLON
    angle = phase * (2.0 * math.pi / NLON)
    pair = np.stack([np.cos(angle), -np.sin(angle)], axis=-1).reshape(NLON, 2 * MT)
    pair = (pair * math.sqrt(2.0 / NLON)).astype(np.float32).astype(ml_dtypes.bfloat16)
    return np.ascontiguousarray(pair.reshape(NLON, 2, MT).transpose(1, 0, 2))


def latitude_constant():
    phase = (np.arange(NDEG)[None, :] * (2 * np.arange(NLAT)[:, None] + 1)) % (4 * NLAT)
    basis = np.cos(phase * (math.pi / (2 * NLAT))) * math.sqrt(2.0 / NLAT)
    padded = np.zeros((2, HALF, 16, NDEG), np.float32)
    padded[:, :, :CYC] = basis.reshape(2, HALF, CYC, NDEG)
    return padded.reshape(2, HALF * 16, NDEG).astype(ml_dtypes.bfloat16)


def spread_constant():
    place = np.zeros((16 * 24, 16 * 32), np.float32)
    for d in range(16):
        place[d * 24 + np.arange(24), d * 32 + np.arange(24)] = 1.0
    return place.astype(ml_dtypes.bfloat16)


def order_constant():
    order = np.zeros((64, 48), np.float32)
    for e in range(2):
        for l in range(2):
            for j in range(CYC):
                order[(2 * e + l) * 16 + j, e * 24 + 2 * j + l] = 1.0
    return order.astype(ml_dtypes.bfloat16)


def kernel(
    trees,
    weight_h, grad_h, pert_h, band_h, wave_h, spec_h, table_h, basis_h, place_h, order_h,
    out_ref,
    weight_s, grad_v, pert_v, band_v, wave_v, spec_v, table_v, basis_v, place_v, order_v,
    gpack, area, factor, gbuf, alpha, zsend, zrecv, send, recv,
    load_sem, gs_sem, gr_sem, as_sem, ar_sem, bs_sem, br_sem, ready,
):
    m = lax.axis_index("mem")
    space = lax.axis_index("space")
    zh = space // HALF
    s32 = space % HALF
    z = zh * MEMS + m

    def along(d, place=None):
        to = (z + d + RING) % RING
        return to % MEMS, to // MEMS * HALF + (s32 if place is None else place)

    loads = [
        (grad_h.reshape(ROWS, 192), grad_v), (band_h, band_v), (wave_h, wave_v), (spec_h, spec_v),
        (pert_h.reshape(2, ROWS, NLON), pert_v), (table_h.at[1 - zh], table_v.at[0]),
        (table_h.at[zh], table_v.at[1]), (place_h, place_v), (basis_h.at[zh], basis_v.at[0]),
        (basis_h.at[1 - zh], basis_v.at[1]), (order_h, order_v), (weight_h, weight_s),
    ]
    loads = [pltpu.make_async_copy(a, b, load_sem.at[i]) for i, (a, b) in enumerate(loads)]
    loads[0].start()

    barrier = pltpu.get_barrier_semaphore()
    for d in (4, -4, 3, -3, 2, -2, 1, -1):
        pl.semaphore_signal(barrier, inc=1, device_id=along(d), device_id_type=MESH)

    def greet_half(d, _):
        pl.semaphore_signal(
            barrier, inc=1, device_id=(m, zh * HALF + (s32 + d) % HALF), device_id_type=MESH
        )
        return 0

    lax.fori_loop(1, HALF, greet_half, 0)
    for c in [loads[11]] + loads[1:11]:
        c.start()

    loads[0].wait()
    gpack[:, 0:192] = grad_v[...].astype(F32)
    lane = lax.broadcasted_iota(jnp.int32, (ROWS, 128), 1)
    low = lane < 64
    t0 = gpack[:, 0:128]
    t1 = gpack[:, 128:256]
    odd = m % 2
    full = jnp.where(odd == 1, jnp.where(low, pltpu.roll(t0, 64, 1), pltpu.roll(t1, 64, 1)), t0)
    part = jnp.where(odd == 1, t0, t1)
    turned = pltpu.roll(part, 64, 1)
    low72 = low[0:72]
    folded = jnp.where(
        odd == 1,
        jnp.where(low72, part[72:144], turned[0:72]),
        jnp.where(low72, part[0:72], turned[72:144]),
    )
    gbuf[m, 0:144] = full.astype(BF16)
    gbuf[m, 144:224] = jnp.concatenate([folded, jnp.zeros((8, 128), F32)], axis=0).astype(BF16)

    pl.semaphore_wait(barrier, 2 * REACH + HALF - 1)

    def gather_copy(s, child, index):
        return pltpu.make_async_remote_copy(
            gbuf.at[s], gbuf.at[s], gs_sem.at[index], gr_sem.at[s],
            device_id=(child, space), device_id_type=MESH,
        )

    children, depths = trees
    for k in range(MEMS):
        @pl.when(m == k)
        def _(k=k):
            for i, c in enumerate(children[k][k]):
                gather_copy(k, c, i).start()

    pl.semaphore_signal(ready, inc=1, device_id=along(-4), device_id_type=MESH)

    loads[1].wait()
    loads[11].wait()
    band = band_v[...]
    a = jnp.zeros((CYC, NLON), F32)
    for b in range(16):
        a = jnp.where(band == b, weight_s[b], a)
    for j in range(CYC):
        area[2 * j : 2 * j + 2] = jnp.broadcast_to(a[j : j + 1], (2, NLON))

    loads[2].wait()
    loads[3].wait()
    for t in range(6):
        idx = wave_v[:, t * 128 : t * 128 + 128]
        block = idx // 128
        place = idx % 128
        for l in range(2):
            got = jnp.zeros((CYC, 128), F32)
            for b in range(6):
                row = jnp.broadcast_to(spec_v[l : l + 1, b * 128 : b * 128 + 128], (CYC, 128))
                got = jnp.where(block == b, jnp.take_along_axis(row, place, axis=1), got)
            for r in range(CYC):
                factor[l, 2 * r : 2 * r + 2, t * 128 : t * 128 + 128] = jnp.broadcast_to(
                    got[r : r + 1], (2, 128)
                )

    def passes(k):
        order = [s for s in range(MEMS) if s != k and children[s][k]]
        order.sort(key=lambda s: (depths[s][k], abs(s - k)))
        return order, [s for s in range(MEMS) if s != k and not children[s][k]]

    for k in range(MEMS):
        @pl.when(m == k)
        def _(k=k):
            count = len(children[k][k])
            through, last = passes(k)
            for s in through:
                gather_copy(s, 0, 0).wait_recv()
                for c in children[s][k]:
                    gather_copy(s, c, count).start()
                    count += 1
            for s in last:
                gather_copy(s, 0, 0).wait_recv()

    loads[4].wait()
    low = low72
    for p in range(4):
        ge = gbuf[2 * p].astype(F32)
        go = gbuf[2 * p + 1].astype(F32)
        fe, fo = ge[144:216], go[144:216]
        mid = jnp.concatenate(
            [jnp.where(low, fe, fo), pltpu.roll(jnp.where(low, fo, fe), 64, 1)], axis=0
        )
        for t, tile in enumerate((ge[0:144], mid, go[0:144])):
            lanes = slice((3 * p + t) * 128, (3 * p + t) * 128 + 128)
            rows = []
            for e in range(2):
                pert = pert_v[e, :, lanes].astype(F32)
                acc = pert[0:24] * tile[0:24]
                for f in range(1, FIELDS):
                    acc = acc + pert[f * 24 : f * 24 + 24] * tile[f * 24 : f * 24 + 24]
                rows.append(area[:, lanes] * acc)
            alpha[:, lanes] = jnp.concatenate(rows, axis=0).astype(BF16)

    pl.semaphore_wait(ready, 1)
    across = [
        pltpu.make_async_remote_copy(
            zsend.at[i], zrecv.at[i], as_sem.at[i], ar_sem.at[i],
            device_id=along(8), device_id_type=MESH,
        )
        for i in range(2)
    ]
    for i in range(5, 11):
        loads[i].wait()

    def cross_over():
        for i in range(2):
            part = jnp.dot(
                alpha[...], table_v[0, :, i * 384 : i * 384 + 384], preferred_element_type=F32
            )
            zsend[i] = part.astype(BF16)
            across[i].start()

    lane = lax.broadcasted_iota(jnp.int32, (16, 128), 1)

    def message(kind, slot):
        return pltpu.make_async_remote_copy(
            send.at[kind, slot], recv.at[kind, s32], bs_sem.at[kind], br_sem.at[kind],
            device_id=(m, zh * HALF + slot), device_id_type=MESH,
        )

    def spread(part, kind, base):
        part = jnp.dot(order_v[...], part, preferred_element_type=F32).astype(BF16)
        y = jnp.dot(part, place_v[...], preferred_element_type=F32)
        for t in range(4):
            blocks = [y[16 * el : 16 * el + 16, t * 128 : t * 128 + 128] for el in range(4)]
            for d in range(4):
                whole = None
                for el in range(4):
                    shift = (32 * (el - d)) % 128
                    moved = pltpu.roll(blocks[el], shift, 1) if shift else blocks[el]
                    whole = moved if whole is None else jnp.where(lane >= 32 * el, moved, whole)
                slot = base + 4 * t + d
                send[kind, slot] = whole.astype(BF16)

                @pl.when(s32 != slot)
                def _(slot=slot):
                    message(kind, slot).start()

    def arrived(kind, sem):
        count = HALF - 1
        pltpu.make_async_copy(send.at[kind, 0:count], recv.at[kind, 0:count], sem.at[kind]).wait()

    def keep():
        mine = jnp.dot(alpha[...], table_v[1], preferred_element_type=F32).astype(BF16)
        spread(mine[:, 0:384], 0, 0)
        spread(mine[:, 384:768], 0, 16)
        recv[0, s32] = send[0, s32]

    early = zh == 1
    pl.when(early)(cross_over)
    keep()
    pl.when(jnp.logical_not(early))(cross_over)
    for i in range(2):
        across[i].wait_recv()
        spread(zrecv[i], 1, 16 * i)

    recv[1, s32] = send[1, s32]
    arrived(0, br_sem)
    dims = (((0,), (0,)), ((), ()))
    total = lax.dot_general(
        recv[0].reshape(HALF * 16, 128), basis_v[0], dims, preferred_element_type=F32
    )
    arrived(1, br_sem)
    total = total + lax.dot_general(
        recv[1].reshape(HALF * 16, 128), basis_v[1], dims, preferred_element_type=F32
    )
    for e in range(2):
        for l in range(2):
            el = 2 * e + l
            out_ref[e, l] = total[el * 32 : el * 32 + 24] * factor[l]

    for k in range(MEMS):
        @pl.when(m == k)
        def _(k=k):
            count = 0
            for s in [k] + passes(k)[0]:
                for c in children[s][k]:
                    gather_copy(s, c, count).wait_send()
                    count += 1
    for i in range(2):
        across[i].wait_send()
    arrived(0, bs_sem)
    arrived(1, bs_sem)


def body(gradient, perturbations, band_index, band_weight, wave_index, spectrum):
    trees = gather_trees()
    table = jnp.asarray(zonal_constant())
    basis = jnp.asarray(latitude_constant())
    place = jnp.asarray(spread_constant())
    order = jnp.asarray(order_constant())
    gradient = gradient.transpose(0, 2, 1, 3)
    perturbations = perturbations.transpose(0, 1, 3, 2, 4)
    hbm = pl.BlockSpec(memory_space=pl.ANY)
    dma = pltpu.SemaphoreType.DMA
    return pl.pallas_call(
        functools.partial(kernel, trees),
        name="alpha_adjoint",
        out_shape=pltpu.VMEM((2, 2, 24, NDEG), F32),
        in_specs=[hbm] * 10,
        out_specs=pl.BlockSpec(memory_space=pltpu.VMEM),
        scratch_shapes=[
            pltpu.SMEM(band_weight.shape, F32),
            pltpu.VMEM((ROWS, 192), BF16),
            pltpu.VMEM((2, ROWS, NLON), BF16),
            pltpu.VMEM(band_index.shape, jnp.int32),
            pltpu.VMEM(wave_index.shape, jnp.int32),
            pltpu.VMEM(spectrum.shape, F32),
            pltpu.VMEM(table.shape, BF16),
            pltpu.VMEM(basis.shape, BF16),
            pltpu.VMEM(place.shape, BF16),
            pltpu.VMEM(order.shape, BF16),
            pltpu.VMEM((ROWS, 256), F32),
            pltpu.VMEM((24, NLON), F32),
            pltpu.VMEM((2, 24, NDEG), F32),
            pltpu.VMEM((MEMS, GROWS, 128), BF16),
            pltpu.VMEM((48, NLON), BF16),
            pltpu.VMEM((2, 48, 384), BF16),
            pltpu.VMEM((2, 48, 384), BF16),
            pltpu.VMEM((2, HALF, 16, 128), BF16),
            pltpu.VMEM((2, HALF, 16, 128), BF16),
            dma((12,)),
            dma((24,)),
            dma((MEMS,)),
            dma((2,)),
            dma((2,)),
            dma((2,)),
            dma((2,)),
            pltpu.SemaphoreType.REGULAR,
        ],
        compiler_params=pltpu.CompilerParams(
            collective_id=0, has_side_effects=True, vmem_limit_bytes=60 * 2**20
        ),
    )(band_weight, gradient, perturbations, band_index, wave_index, spectrum, table, basis, place, order)


def solution(mesh):
    in_specs = (
        P(None, None, "space", "mem"),
        P("mem", None, None, "space", None),
        P("space", None),
        P(),
        P("space", None),
        P(),
    )
    out_specs = P("mem", None, "space", None)
    return jax.shard_map(body, mesh=mesh, in_specs=in_specs, out_specs=out_specs, check_vma=False)
```

```python
import functools
import math

import jax
import jax.numpy as jnp
import ml_dtypes
import numpy as np
from jax import lax
from jax.experimental import pallas as pl
from jax.experimental.pallas import tpu as pltpu
from jax.sharding import PartitionSpec as P

MESH = pl.DeviceIdType.MESH
BF16 = jnp.bfloat16
F32 = jnp.float32

MEMS = 8
HALF = 32
NLAT = 768
NLON = 1536
MT = 768
NDEG = 768
CYC = 12
FIELDS = 6
ROWS = 144
GROWS = 224
REACH = 4
RING = 16

PARENTS = (
    (0, 0, 0, 2, 0, 4, 4, 4),
    (1, 1, 1, 2, 5, 1, 5, 5),
    (1, 2, 2, 2, 6, 6, 2, 6),
    (1, 3, 3, 3, 7, 7, 7, 3),
    (4, 0, 0, 0, 4, 4, 4, 6),
    (1, 5, 1, 1, 5, 5, 5, 6),
    (2, 2, 6, 2, 5, 6, 6, 6),
    (3, 3, 3, 7, 5, 7, 7, 7),
)


def gather_trees():
    parents = PARENTS
    children = [
        [[c for c in range(MEMS) if c != s and parents[s][c] == n] for n in range(MEMS)] for s in range(MEMS)
    ]
    depths = []
    for s in range(MEMS):
        row = []
        for n in range(MEMS):
            depth = 0
            while n != s:
                assert abs(n - parents[s][n]) <= REACH
                n = parents[s][n]
                depth += 1
            row.append(depth)
        depths.append(row)
    for s in range(MEMS):
        for n in range(MEMS):
            children[s][n].sort(key=lambda c: (-len(children[s][c]), c))
    return children, depths


def zonal_constant():
    phase = (np.arange(NLON)[:, None] * np.arange(MT)[None, :]) % NLON
    angle = phase * (2.0 * math.pi / NLON)
    pair = np.stack([np.cos(angle), -np.sin(angle)], axis=-1).reshape(NLON, 2 * MT)
    pair = (pair * math.sqrt(2.0 / NLON)).astype(np.float32).astype(ml_dtypes.bfloat16)
    return np.ascontiguousarray(pair.reshape(NLON, 2, MT).transpose(1, 0, 2))


def latitude_constant():
    phase = (np.arange(NDEG)[None, :] * (2 * np.arange(NLAT)[:, None] + 1)) % (4 * NLAT)
    basis = np.cos(phase * (math.pi / (2 * NLAT))) * math.sqrt(2.0 / NLAT)
    padded = np.zeros((2, HALF, 16, NDEG), np.float32)
    padded[:, :, :CYC] = basis.reshape(2, HALF, CYC, NDEG)
    return padded.reshape(2, HALF * 16, NDEG).astype(ml_dtypes.bfloat16)


def spread_constant():
    place = np.zeros((16 * 24, 16 * 32), np.float32)
    for d in range(16):
        place[d * 24 + np.arange(24), d * 32 + np.arange(24)] = 1.0
    return place.astype(ml_dtypes.bfloat16)


def order_constant():
    order = np.zeros((64, 48), np.float32)
    for e in range(2):
        for l in range(2):
            for j in range(CYC):
                order[(2 * e + l) * 16 + j, e * 24 + 2 * j + l] = 1.0
    return order.astype(ml_dtypes.bfloat16)


def kernel(
    trees,
    weight_h, grad_h, pert_h, band_h, wave_h, spec_h, table_h, basis_h, place_h, order_h,
    out_ref,
    weight_s, grad_v, pert_v, band_v, wave_v, spec_v, table_v, basis_v, place_v, order_v,
    gpack, area, factor, gbuf, alpha, zsend, zrecv, send, recv,
    load_sem, gs_sem, gr_sem, as_sem, ar_sem, bs_sem, br_sem, ready,
):
    m = lax.axis_index("mem")
    space = lax.axis_index("space")
    zh = space // HALF
    s32 = space % HALF
    z = zh * MEMS + m

    def along(d, place=None):
        to = (z + d + RING) % RING
        return to % MEMS, to // MEMS * HALF + (s32 if place is None else place)

    loads = [
        (grad_h.reshape(ROWS, 192), grad_v), (band_h, band_v), (wave_h, wave_v), (spec_h, spec_v),
        (pert_h.reshape(2, ROWS, NLON), pert_v), (table_h.at[1 - zh], table_v.at[0]),
        (table_h.at[zh], table_v.at[1]), (place_h, place_v), (basis_h.at[zh], basis_v.at[0]),
        (basis_h.at[1 - zh], basis_v.at[1]), (order_h, order_v), (weight_h, weight_s),
    ]
    loads = [pltpu.make_async_copy(a, b, load_sem.at[i]) for i, (a, b) in enumerate(loads)]
    loads[0].start()

    barrier = pltpu.get_barrier_semaphore()
    for d in (4, -4, 3, -3, 2, -2, 1, -1):
        pl.semaphore_signal(barrier, inc=1, device_id=along(d), device_id_type=MESH)

    def greet_half(d, _):
        pl.semaphore_signal(
            barrier, inc=1, device_id=(m, zh * HALF + (s32 + d) % HALF), device_id_type=MESH
        )
        return 0

    lax.fori_loop(1, HALF, greet_half, 0)
    for c in [loads[11]] + loads[1:11]:
        c.start()

    loads[0].wait()
    gpack[:, 0:192] = grad_v[...].astype(F32)
    lane = lax.broadcasted_iota(jnp.int32, (ROWS, 128), 1)
    low = lane < 64
    t0 = gpack[:, 0:128]
    t1 = gpack[:, 128:256]
    odd = m % 2
    full = jnp.where(odd == 1, jnp.where(low, pltpu.roll(t0, 64, 1), pltpu.roll(t1, 64, 1)), t0)
    part = jnp.where(odd == 1, t0, t1)
    turned = pltpu.roll(part, 64, 1)
    low72 = low[0:72]
    folded = jnp.where(
        odd == 1,
        jnp.where(low72, part[72:144], turned[0:72]),
        jnp.where(low72, part[0:72], turned[72:144]),
    )
    gbuf[m, 0:144] = full.astype(BF16)
    gbuf[m, 144:224] = jnp.concatenate([folded, jnp.zeros((8, 128), F32)], axis=0).astype(BF16)

    pl.semaphore_wait(barrier, 2 * REACH + HALF - 1)

    def gather_copy(s, child, index):
        return pltpu.make_async_remote_copy(
            gbuf.at[s], gbuf.at[s], gs_sem.at[index], gr_sem.at[s],
            device_id=(child, space), device_id_type=MESH,
        )

    children, depths = trees
    for k in range(MEMS):
        @pl.when(m == k)
        def _(k=k):
            for i, c in enumerate(children[k][k]):
                gather_copy(k, c, i).start()

    pl.semaphore_signal(ready, inc=1, device_id=along(-4), device_id_type=MESH)

    loads[1].wait()
    loads[11].wait()
    band = band_v[...]
    a = jnp.zeros((CYC, NLON), F32)
    for b in range(16):
        a = jnp.where(band == b, weight_s[b], a)
    for j in range(CYC):
        area[2 * j : 2 * j + 2] = jnp.broadcast_to(a[j : j + 1], (2, NLON))

    loads[2].wait()
    loads[3].wait()
    for t in range(6):
        idx = wave_v[:, t * 128 : t * 128 + 128]
        block = idx // 128
        place = idx % 128
        for l in range(2):
            got = jnp.zeros((CYC, 128), F32)
            for b in range(6):
                row = jnp.broadcast_to(spec_v[l : l + 1, b * 128 : b * 128 + 128], (CYC, 128))
                got = jnp.where(block == b, jnp.take_along_axis(row, place, axis=1), got)
            for r in range(CYC):
                factor[l, 2 * r : 2 * r + 2, t * 128 : t * 128 + 128] = jnp.broadcast_to(
                    got[r : r + 1], (2, 128)
                )

    def passes(k):
        order = [s for s in range(MEMS) if s != k and children[s][k]]
        order.sort(key=lambda s: (depths[s][k], abs(s - k)))
        return order, [s for s in range(MEMS) if s != k and not children[s][k]]

    for k in range(MEMS):
        @pl.when(m == k)
        def _(k=k):
            count = len(children[k][k])
            through, last = passes(k)
            for s in through:
                gather_copy(s, 0, 0).wait_recv()
                for c in children[s][k]:
                    gather_copy(s, c, count).start()
                    count += 1
            for s in last:
                gather_copy(s, 0, 0).wait_recv()

    loads[4].wait()
    low = low72
    for p in range(4):
        ge = gbuf[2 * p].astype(F32)
        go = gbuf[2 * p + 1].astype(F32)
        fe, fo = ge[144:216], go[144:216]
        mid = jnp.concatenate(
            [jnp.where(low, fe, fo), pltpu.roll(jnp.where(low, fo, fe), 64, 1)], axis=0
        )
        for t, tile in enumerate((ge[0:144], mid, go[0:144])):
            lanes = slice((3 * p + t) * 128, (3 * p + t) * 128 + 128)
            rows = []
            for e in range(2):
                pert = pert_v[e, :, lanes].astype(F32)
                acc = pert[0:24] * tile[0:24]
                for f in range(1, FIELDS):
                    acc = acc + pert[f * 24 : f * 24 + 24] * tile[f * 24 : f * 24 + 24]
                rows.append(area[:, lanes] * acc)
            alpha[:, lanes] = jnp.concatenate(rows, axis=0).astype(BF16)

    pl.semaphore_wait(ready, 1)
    across = [
        pltpu.make_async_remote_copy(
            zsend.at[i], zrecv.at[i], as_sem.at[i], ar_sem.at[i],
            device_id=along(8), device_id_type=MESH,
        )
        for i in range(2)
    ]
    for i in range(5, 11):
        loads[i].wait()

    def cross_over():
        for i in range(2):
            part = jnp.dot(
                alpha[...], table_v[0, :, i * 384 : i * 384 + 384], preferred_element_type=F32
            )
            zsend[i] = part.astype(BF16)
            across[i].start()

    lane = lax.broadcasted_iota(jnp.int32, (16, 128), 1)

    def message(kind, slot):
        return pltpu.make_async_remote_copy(
            send.at[kind, slot], recv.at[kind, s32], bs_sem.at[kind], br_sem.at[kind],
            device_id=(m, zh * HALF + slot), device_id_type=MESH,
        )

    def spread(part, kind, base):
        part = jnp.dot(order_v[...], part, preferred_element_type=F32).astype(BF16)
        y = jnp.dot(part, place_v[...], preferred_element_type=F32)
        for t in range(4):
            blocks = [y[16 * el : 16 * el + 16, t * 128 : t * 128 + 128] for el in range(4)]
            for d in range(4):
                whole = None
                for el in range(4):
                    shift = (32 * (el - d)) % 128
                    moved = pltpu.roll(blocks[el], shift, 1) if shift else blocks[el]
                    whole = moved if whole is None else jnp.where(lane >= 32 * el, moved, whole)
                slot = base + 4 * t + d
                send[kind, slot] = whole.astype(BF16)

                @pl.when(s32 != slot)
                def _(slot=slot):
                    message(kind, slot).start()

    def arrived(kind, sem):
        count = HALF - 1
        pltpu.make_async_copy(send.at[kind, 0:count], recv.at[kind, 0:count], sem.at[kind]).wait()

    def keep():
        mine = jnp.dot(alpha[...], table_v[1], preferred_element_type=F32).astype(BF16)
        spread(mine[:, 0:384], 0, 0)
        spread(mine[:, 384:768], 0, 16)
        recv[0, s32] = send[0, s32]

    early = zh == 1
    pl.when(early)(cross_over)
    keep()
    pl.when(jnp.logical_not(early))(cross_over)
    for i in range(2):
        across[i].wait_recv()
        spread(zrecv[i], 1, 16 * i)

    recv[1, s32] = send[1, s32]
    arrived(0, br_sem)
    dims = (((0,), (0,)), ((), ()))
    total = lax.dot_general(
        recv[0].reshape(HALF * 16, 128), basis_v[0], dims, preferred_element_type=F32
    )
    arrived(1, br_sem)
    total = total + lax.dot_general(
        recv[1].reshape(HALF * 16, 128), basis_v[1], dims, preferred_element_type=F32
    )
    for e in range(2):
        for l in range(2):
            el = 2 * e + l
            out_ref[e, l] = total[el * 32 : el * 32 + 24] * factor[l]

    for k in range(MEMS):
        @pl.when(m == k)
        def _(k=k):
            count = 0
            for s in [k] + passes(k)[0]:
                for c in children[s][k]:
                    gather_copy(s, c, count).wait_send()
                    count += 1
    for i in range(2):
        across[i].wait_send()
    arrived(0, bs_sem)
    arrived(1, bs_sem)


def body(gradient, perturbations, band_index, band_weight, wave_index, spectrum):
    trees = gather_trees()
    table = jnp.asarray(zonal_constant())
    basis = jnp.asarray(latitude_constant())
    place = jnp.asarray(spread_constant())
    order = jnp.asarray(order_constant())
    gradient = gradient.transpose(0, 2, 1, 3)
    perturbations = perturbations.transpose(0, 1, 3, 2, 4)
    hbm = pl.BlockSpec(memory_space=pl.ANY)
    dma = pltpu.SemaphoreType.DMA
    return pl.pallas_call(
        functools.partial(kernel, trees),
        name="alpha_adjoint",
        out_shape=pltpu.VMEM((2, 2, 24, NDEG), F32),
        in_specs=[hbm] * 10,
        out_specs=pl.BlockSpec(memory_space=pltpu.VMEM),
        scratch_shapes=[
            pltpu.SMEM(band_weight.shape, F32),
            pltpu.VMEM((ROWS, 192), BF16),
            pltpu.VMEM((2, ROWS, NLON), BF16),
            pltpu.VMEM(band_index.shape, jnp.int32),
            pltpu.VMEM(wave_index.shape, jnp.int32),
            pltpu.VMEM(spectrum.shape, F32),
            pltpu.VMEM(table.shape, BF16),
            pltpu.VMEM(basis.shape, BF16),
            pltpu.VMEM(place.shape, BF16),
            pltpu.VMEM(order.shape, BF16),
            pltpu.VMEM((ROWS, 256), F32),
            pltpu.VMEM((24, NLON), F32),
            pltpu.VMEM((2, 24, NDEG), F32),
            pltpu.VMEM((MEMS, GROWS, 128), BF16),
            pltpu.VMEM((48, NLON), BF16),
            pltpu.VMEM((2, 48, 384), BF16),
            pltpu.VMEM((2, 48, 384), BF16),
            pltpu.VMEM((2, HALF, 16, 128), BF16),
            pltpu.VMEM((2, HALF, 16, 128), BF16),
            dma((12,)),
            dma((24,)),
            dma((MEMS,)),
            dma((2,)),
            dma((2,)),
            dma((2,)),
            dma((2,)),
            pltpu.SemaphoreType.REGULAR,
        ],
        compiler_params=pltpu.CompilerParams(
            collective_id=0, has_side_effects=True, vmem_limit_bytes=60 * 2**20
        ),
    )(band_weight, gradient, perturbations, band_index, wave_index, spectrum, table, basis, place, order)


def solution(mesh):
    in_specs = (
        P(None, None, "space", "mem"),
        P("mem", None, None, "space", None),
        P("space", None),
        P(),
        P("space", None),
        P(),
    )
    out_specs = P("mem", None, "space", None)
    return jax.shard_map(body, mesh=mesh, in_specs=in_specs, out_specs=out_specs, check_vma=False)
```

```python
import functools
import math

import jax
import jax.numpy as jnp
import ml_dtypes
import numpy as np
from jax import lax
from jax.experimental import pallas as pl
from jax.experimental.pallas import tpu as pltpu
from jax.sharding import PartitionSpec as P

MESH = pl.DeviceIdType.MESH
BF16 = jnp.bfloat16
F32 = jnp.float32

MEMS = 8
HALF = 32
NLAT = 768
NLON = 1536
MT = 768
NDEG = 768
CYC = 12
FIELDS = 6
ROWS = 144
GROWS = 224
REACH = 4
RING = 16

PARENTS = (
    (0, 0, 0, 2, 0, 4, 4, 4),
    (1, 1, 1, 2, 5, 1, 5, 5),
    (1, 2, 2, 2, 6, 6, 2, 6),
    (1, 3, 3, 3, 7, 7, 7, 3),
    (4, 0, 0, 0, 4, 4, 4, 6),
    (1, 5, 1, 1, 5, 5, 5, 6),
    (2, 2, 6, 2, 5, 6, 6, 6),
    (3, 3, 3, 7, 5, 7, 7, 7),
)


def gather_trees():
    parents = PARENTS
    children = [
        [[c for c in range(MEMS) if c != s and parents[s][c] == n] for n in range(MEMS)] for s in range(MEMS)
    ]
    depths = []
    for s in range(MEMS):
        row = []
        for n in range(MEMS):
            depth = 0
            while n != s:
                assert abs(n - parents[s][n]) <= REACH
                n = parents[s][n]
                depth += 1
            row.append(depth)
        depths.append(row)
    for s in range(MEMS):
        for n in range(MEMS):
            children[s][n].sort(key=lambda c: (-len(children[s][c]), c))
    return children, depths


def zonal_constant():
    phase = (np.arange(NLON)[:, None] * np.arange(MT)[None, :]) % NLON
    angle = phase * (2.0 * math.pi / NLON)
    pair = np.stack([np.cos(angle), -np.sin(angle)], axis=-1).reshape(NLON, 2 * MT)
    pair = (pair * math.sqrt(2.0 / NLON)).astype(np.float32).astype(ml_dtypes.bfloat16)
    return np.ascontiguousarray(pair.reshape(NLON, 2, MT).transpose(1, 0, 2))


def latitude_constant():
    phase = (np.arange(NDEG)[None, :] * (2 * np.arange(NLAT)[:, None] + 1)) % (4 * NLAT)
    basis = np.cos(phase * (math.pi / (2 * NLAT))) * math.sqrt(2.0 / NLAT)
    padded = np.zeros((2, HALF, 16, NDEG), np.float32)
    padded[:, :, :CYC] = basis.reshape(2, HALF, CYC, NDEG)
    return padded.reshape(2, HALF * 16, NDEG).astype(ml_dtypes.bfloat16)


def spread_constant():
    place = np.zeros((16 * 24, 16 * 32), np.float32)
    for d in range(16):
        place[d * 24 + np.arange(24), d * 32 + np.arange(24)] = 1.0
    return place.astype(ml_dtypes.bfloat16)


def order_constant():
    order = np.zeros((64, 48), np.float32)
    for e in range(2):
        for l in range(2):
            for j in range(CYC):
                order[(2 * e + l) * 16 + j, e * 24 + 2 * j + l] = 1.0
    return order.astype(ml_dtypes.bfloat16)


def kernel(
    trees,
    weight_h, grad_h, pert_h, band_h, wave_h, spec_h, table_h, basis_h, place_h, order_h,
    out_ref,
    weight_s, grad_v, pert_v, band_v, wave_v, spec_v, table_v, basis_v, place_v, order_v,
    gpack, area, factor, gbuf, alpha, zsend, zrecv, send, recv,
    load_sem, gs_sem, gr_sem, as_sem, ar_sem, bs_sem, br_sem, ready,
):
    m = lax.axis_index("mem")
    space = lax.axis_index("space")
    zh = space // HALF
    s32 = space % HALF
    z = zh * MEMS + m

    def along(d, place=None):
        to = (z + d + RING) % RING
        return to % MEMS, to // MEMS * HALF + (s32 if place is None else place)

    loads = [
        (grad_h.reshape(ROWS, 192), grad_v), (band_h, band_v), (wave_h, wave_v), (spec_h, spec_v),
        (pert_h.reshape(2, ROWS, NLON), pert_v), (table_h.at[1 - zh], table_v.at[0]),
        (table_h.at[zh], table_v.at[1]), (place_h, place_v), (basis_h.at[zh], basis_v.at[0]),
        (basis_h.at[1 - zh], basis_v.at[1]), (order_h, order_v), (weight_h, weight_s),
    ]
    loads = [pltpu.make_async_copy(a, b, load_sem.at[i]) for i, (a, b) in enumerate(loads)]
    loads[0].start()

    barrier = pltpu.get_barrier_semaphore()
    for d in (4, -4, 3, -3, 2, -2, 1, -1):
        pl.semaphore_signal(barrier, inc=1, device_id=along(d), device_id_type=MESH)

    def greet_half(d, _):
        pl.semaphore_signal(
            barrier, inc=1, device_id=(m, zh * HALF + (s32 + d) % HALF), device_id_type=MESH
        )
        return 0

    lax.fori_loop(1, HALF, greet_half, 0)
    loads[0].wait()
    gpack[:, 0:192] = grad_v[...].astype(F32)
    lane = lax.broadcasted_iota(jnp.int32, (ROWS, 128), 1)
    low = lane < 64
    t0 = gpack[:, 0:128]
    t1 = gpack[:, 128:256]
    odd = m % 2
    full = jnp.where(odd == 1, jnp.where(low, pltpu.roll(t0, 64, 1), pltpu.roll(t1, 64, 1)), t0)
    part = jnp.where(odd == 1, t0, t1)
    turned = pltpu.roll(part, 64, 1)
    low72 = low[0:72]
    folded = jnp.where(
        odd == 1,
        jnp.where(low72, part[72:144], turned[0:72]),
        jnp.where(low72, part[0:72], turned[72:144]),
    )
    gbuf[m, 0:144] = full.astype(BF16)
    gbuf[m, 144:224] = jnp.concatenate([folded, jnp.zeros((8, 128), F32)], axis=0).astype(BF16)

    pl.semaphore_wait(barrier, 2 * REACH + HALF - 1)

    def gather_copy(s, child, index):
        return pltpu.make_async_remote_copy(
            gbuf.at[s], gbuf.at[s], gs_sem.at[index], gr_sem.at[s],
            device_id=(child, space), device_id_type=MESH,
        )

    children, depths = trees
    for k in range(MEMS):
        @pl.when(m == k)
        def _(k=k):
            for i, c in enumerate(children[k][k]):
                gather_copy(k, c, i).start()

    pl.semaphore_signal(ready, inc=1, device_id=along(-4), device_id_type=MESH)

    for c in [loads[11]] + loads[1:11]:
        c.start()

    loads[1].wait()
    loads[11].wait()
    band = band_v[...]
    a = jnp.zeros((CYC, NLON), F32)
    for b in range(16):
        a = jnp.where(band == b, weight_s[b], a)
    for j in range(CYC):
        area[2 * j : 2 * j + 2] = jnp.broadcast_to(a[j : j + 1], (2, NLON))

    loads[2].wait()
    loads[3].wait()
    for t in range(6):
        idx = wave_v[:, t * 128 : t * 128 + 128]
        block = idx // 128
        place = idx % 128
        for l in range(2):
            got = jnp.zeros((CYC, 128), F32)
            for b in range(6):
                row = jnp.broadcast_to(spec_v[l : l + 1, b * 128 : b * 128 + 128], (CYC, 128))
                got = jnp.where(block == b, jnp.take_along_axis(row, place, axis=1), got)
            for r in range(CYC):
                factor[l, 2 * r : 2 * r + 2, t * 128 : t * 128 + 128] = jnp.broadcast_to(
                    got[r : r + 1], (2, 128)
                )

    def passes(k):
        order = [s for s in range(MEMS) if s != k and children[s][k]]
        order.sort(key=lambda s: (depths[s][k], abs(s - k)))
        return order, [s for s in range(MEMS) if s != k and not children[s][k]]

    for k in range(MEMS):
        @pl.when(m == k)
        def _(k=k):
            count = len(children[k][k])
            through, last = passes(k)
            for s in through:
                gather_copy(s, 0, 0).wait_recv()
                for c in children[s][k]:
                    gather_copy(s, c, count).start()
                    count += 1
            for s in last:
                gather_copy(s, 0, 0).wait_recv()

    loads[4].wait()
    low = low72
    for p in range(4):
        ge = gbuf[2 * p].astype(F32)
        go = gbuf[2 * p + 1].astype(F32)
        fe, fo = ge[144:216], go[144:216]
        mid = jnp.concatenate(
            [jnp.where(low, fe, fo), pltpu.roll(jnp.where(low, fo, fe), 64, 1)], axis=0
        )
        for t, tile in enumerate((ge[0:144], mid, go[0:144])):
            lanes = slice((3 * p + t) * 128, (3 * p + t) * 128 + 128)
            rows = []
            for e in range(2):
                pert = pert_v[e, :, lanes].astype(F32)
                acc = pert[0:24] * tile[0:24]
                for f in range(1, FIELDS):
                    acc = acc + pert[f * 24 : f * 24 + 24] * tile[f * 24 : f * 24 + 24]
                rows.append(area[:, lanes] * acc)
            alpha[:, lanes] = jnp.concatenate(rows, axis=0).astype(BF16)

    pl.semaphore_wait(ready, 1)
    across = [
        pltpu.make_async_remote_copy(
            zsend.at[i], zrecv.at[i], as_sem.at[i], ar_sem.at[i],
            device_id=along(8), device_id_type=MESH,
        )
        for i in range(2)
    ]
    for i in range(5, 11):
        loads[i].wait()

    def cross_over():
        for i in range(2):
            part = jnp.dot(
                alpha[...], table_v[0, :, i * 384 : i * 384 + 384], preferred_element_type=F32
            )
            zsend[i] = part.astype(BF16)
            across[i].start()

    lane = lax.broadcasted_iota(jnp.int32, (16, 128), 1)

    def message(kind, slot):
        return pltpu.make_async_remote_copy(
            send.at[kind, slot], recv.at[kind, s32], bs_sem.at[kind], br_sem.at[kind],
            device_id=(m, zh * HALF + slot), device_id_type=MESH,
        )

    def spread(part, kind, base):
        part = jnp.dot(order_v[...], part, preferred_element_type=F32).astype(BF16)
        y = jnp.dot(part, place_v[...], preferred_element_type=F32)
        for t in range(4):
            blocks = [y[16 * el : 16 * el + 16, t * 128 : t * 128 + 128] for el in range(4)]
            for d in range(4):
                whole = None
                for el in range(4):
                    shift = (32 * (el - d)) % 128
                    moved = pltpu.roll(blocks[el], shift, 1) if shift else blocks[el]
                    whole = moved if whole is None else jnp.where(lane >= 32 * el, moved, whole)
                slot = base + 4 * t + d
                send[kind, slot] = whole.astype(BF16)

                @pl.when(s32 != slot)
                def _(slot=slot):
                    message(kind, slot).start()

    def arrived(kind, sem):
        count = HALF - 1
        pltpu.make_async_copy(send.at[kind, 0:count], recv.at[kind, 0:count], sem.at[kind]).wait()

    def keep():
        mine = jnp.dot(alpha[...], table_v[1], preferred_element_type=F32).astype(BF16)
        spread(mine[:, 0:384], 0, 0)
        spread(mine[:, 384:768], 0, 16)
        recv[0, s32] = send[0, s32]

    early = zh == 1
    pl.when(early)(cross_over)
    keep()
    pl.when(jnp.logical_not(early))(cross_over)
    for i in range(2):
        across[i].wait_recv()
        spread(zrecv[i], 1, 16 * i)

    recv[1, s32] = send[1, s32]
    arrived(0, br_sem)
    dims = (((0,), (0,)), ((), ()))
    total = lax.dot_general(
        recv[0].reshape(HALF * 16, 128), basis_v[0], dims, preferred_element_type=F32
    )
    arrived(1, br_sem)
    total = total + lax.dot_general(
        recv[1].reshape(HALF * 16, 128), basis_v[1], dims, preferred_element_type=F32
    )
    for e in range(2):
        for l in range(2):
            el = 2 * e + l
            out_ref[e, l] = total[el * 32 : el * 32 + 24] * factor[l]

    for k in range(MEMS):
        @pl.when(m == k)
        def _(k=k):
            count = 0
            for s in [k] + passes(k)[0]:
                for c in children[s][k]:
                    gather_copy(s, c, count).wait_send()
                    count += 1
    for i in range(2):
        across[i].wait_send()
    arrived(0, bs_sem)
    arrived(1, bs_sem)


def body(gradient, perturbations, band_index, band_weight, wave_index, spectrum):
    trees = gather_trees()
    table = jnp.asarray(zonal_constant())
    basis = jnp.asarray(latitude_constant())
    place = jnp.asarray(spread_constant())
    order = jnp.asarray(order_constant())
    gradient = gradient.transpose(0, 2, 1, 3)
    perturbations = perturbations.transpose(0, 1, 3, 2, 4)
    hbm = pl.BlockSpec(memory_space=pl.ANY)
    dma = pltpu.SemaphoreType.DMA
    return pl.pallas_call(
        functools.partial(kernel, trees),
        name="alpha_adjoint",
        out_shape=pltpu.VMEM((2, 2, 24, NDEG), F32),
        in_specs=[hbm] * 10,
        out_specs=pl.BlockSpec(memory_space=pltpu.VMEM),
        scratch_shapes=[
            pltpu.SMEM(band_weight.shape, F32),
            pltpu.VMEM((ROWS, 192), BF16),
            pltpu.VMEM((2, ROWS, NLON), BF16),
            pltpu.VMEM(band_index.shape, jnp.int32),
            pltpu.VMEM(wave_index.shape, jnp.int32),
            pltpu.VMEM(spectrum.shape, F32),
            pltpu.VMEM(table.shape, BF16),
            pltpu.VMEM(basis.shape, BF16),
            pltpu.VMEM(place.shape, BF16),
            pltpu.VMEM(order.shape, BF16),
            pltpu.VMEM((ROWS, 256), F32),
            pltpu.VMEM((24, NLON), F32),
            pltpu.VMEM((2, 24, NDEG), F32),
            pltpu.VMEM((MEMS, GROWS, 128), BF16),
            pltpu.VMEM((48, NLON), BF16),
            pltpu.VMEM((2, 48, 384), BF16),
            pltpu.VMEM((2, 48, 384), BF16),
            pltpu.VMEM((2, HALF, 16, 128), BF16),
            pltpu.VMEM((2, HALF, 16, 128), BF16),
            dma((12,)),
            dma((24,)),
            dma((MEMS,)),
            dma((2,)),
            dma((2,)),
            dma((2,)),
            dma((2,)),
            pltpu.SemaphoreType.REGULAR,
        ],
        compiler_params=pltpu.CompilerParams(
            collective_id=0, has_side_effects=True, vmem_limit_bytes=60 * 2**20
        ),
    )(band_weight, gradient, perturbations, band_index, wave_index, spectrum, table, basis, place, order)


def solution(mesh):
    in_specs = (
        P(None, None, "space", "mem"),
        P("mem", None, None, "space", None),
        P("space", None),
        P(),
        P("space", None),
        P(),
    )
    out_specs = P("mem", None, "space", None)
    return jax.shard_map(body, mesh=mesh, in_specs=in_specs, out_specs=out_specs, check_vma=False)
```
